32 devices in a mesh: ccd: 8 (over y, x, core), quad: 4 (over z).
Axes of the slice: x: 2, y: 2, z: 4, core: 2. Of those that a mesh axis runs over, the one named last changes fastest.
Arguments:
- template_patches: float32 [8, 4, 512, 512], P('ccd', 'quad'), may hold values from -4 to 4
- intersection: int32 [8, 4, 8], P(None, 'quad'), may hold values from 0 to 7, as said below
- offsets: int32 [8, 4, 8], P(None, 'quad'), may hold values from 0 to 448
- science: float32 [8, 4, 512, 512], P('ccd', 'quad'), may hold values from -16 to 16
- weight: float32 [8, 4, 512, 512], P('ccd', 'quad'), may hold values from 0.5 to 32
- positions: int32 [8, 4, 32, 2], P('ccd', 'quad'), may hold values from 0 to 480, as said below
Outputs:
- difference: float32 [8, 4, 512, 512], P('ccd', 'quad')
The draws below stay inside these ranges and needn't reach their ends.
Inputs may be any that keep to these rules, and one draw needn't show every extreme that they name: `intersection`: the 8 entries of one quadrant name different patches. `positions`: each stamp's first column is a multiple of 32.
All inputs are finite; a program needn't handle non-finite values.
Results may differ from the reference program's by a relative error of at most 0.006.
Values sent between devices are 32-bit elements; how exact they have to be, the bound alone decides.
A program may use at most 192 MiB of HBM per device.

```python
import jax
import jax.numpy as jnp
from jax import lax

PIX = 512
BANDS = 8
BAND_ROWS = 64
RADIUS = 10
NBASIS = 27
NCOEF = 84
STAMP = 32
NSTAMP = 32
NCCD = 8
NQUAD = 4


def common_draw(key):
    popular = jax.random.randint(jax.random.fold_in(key, 101), (NCCD,), 0, 4)
    jitter = jax.random.randint(jax.random.fold_in(key, 102), (NCCD, NQUAD, NCCD), 0, 1 << 20)
    labels = jnp.arange(NCCD, dtype=jnp.int32)
    scores = (popular[None, None, :] * (1 << 20) + jitter) * NCCD + labels[None, None, :]
    intersection = lax.top_k(scores, BANDS)[1].astype(jnp.int32)
    offsets = jax.random.randint(jax.random.fold_in(key, 103), (NCCD, NQUAD, BANDS), 0, PIX - BAND_ROWS + 1)
    shape_full = (NCCD, NQUAD, PIX, PIX)
    template = jnp.clip(jax.random.normal(jax.random.fold_in(key, 104), shape_full, jnp.float32), -4.0, 4.0)
    quad_grid = jnp.broadcast_to(jnp.arange(NQUAD, dtype=jnp.int32)[None, :, None], intersection.shape)

    def one_band(patch_index, quad_index, first_row):
        return lax.dynamic_slice(template, (patch_index, quad_index, first_row, jnp.int32(0)), (1, 1, BAND_ROWS, PIX))[0, 0]
    band_list = jax.vmap(one_band)(intersection.reshape(-1), quad_grid.reshape(-1), offsets.reshape(-1))
    windows = band_list.reshape(shape_full)
    row_index = jnp.arange(PIX, dtype=jnp.float32)
    quad_index = jnp.arange(NQUAD, dtype=jnp.float32)
    up_coord = (quad_index[:, None] * PIX + row_index[None, :] + 0.5) / (NQUAD * PIX) * 2.0 - 1.0
    right_coord = (row_index + 0.5) / PIX * 2.0 - 1.0
    up_full = up_coord[None, :, :, None]
    right_full = right_coord[None, None, None, :]
    ccd_gain = 0.2 * jnp.clip(jax.random.normal(jax.random.fold_in(key, 106), (NCCD,), jnp.float32), -2.0, 2.0)
    main_gain = 0.9 + 0.5 * up_full * up_full + 0.4 * right_full + ccd_gain[:, None, None, None]
    down_shift = jnp.pad(windows[:, :, :-1, :], ((0, 0), (0, 0), (1, 0), (0, 0)))
    side_shift = jnp.pad(windows[:, :, :, :-1], ((0, 0), (0, 0), (0, 0), (1, 0)))
    noise_term = 0.3 * jnp.clip(jax.random.normal(jax.random.fold_in(key, 107), shape_full, jnp.float32), -4.0, 4.0)
    science = main_gain * windows + 0.35 * up_full * down_shift + 0.35 * right_full * side_shift + 0.5 * up_full + 1.5 * right_full + noise_term
    return (intersection, offsets, template, science)


def draw_template_patches(key, part):
    return common_draw(key)[2]


def draw_intersection(key, part):
    return common_draw(key)[0]


def draw_offsets(key, part):
    return common_draw(key)[1]


def draw_science(key, part):
    return common_draw(key)[3]


def draw_weight(key, part):
    key = jax.random.fold_in(key, 5)
    shape_full = (NCCD, NQUAD, PIX, PIX)
    quad_factor = 1.0 + jnp.arange(NQUAD, dtype=jnp.float32) / (NQUAD - 1)
    column_place = (jnp.arange(PIX, dtype=jnp.int32) % STAMP).astype(jnp.float32) / (STAMP - 1)
    column_ramp = jnp.exp(jnp.log(8.0) * column_place)
    base_values = jnp.exp(jax.random.uniform(jax.random.fold_in(key, 201), shape_full, jnp.float32, jnp.log(0.5), jnp.log(2.0)))
    return base_values * quad_factor[None, :, None, None] * column_ramp[None, None, None, :]


def draw_positions(key, part):
    key = jax.random.fold_in(key, 7)
    stamp_rows = jax.random.randint(jax.random.fold_in(key, 301), (NCCD, NQUAD, NSTAMP, 1), 0, PIX - STAMP + 1)
    stamp_cols = STAMP * jax.random.randint(jax.random.fold_in(key, 302), (NCCD, NQUAD, NSTAMP, 1), 0, (PIX - STAMP) // STAMP + 1)
    return jnp.concatenate([stamp_rows, stamp_cols], -1).astype(jnp.int32)


def setup_inputs(seed: int = 0) -> dict:
    key_list = jax.random.split(jax.random.key(seed), 7)
    return {
        "template_patches": draw_template_patches(jax.random.fold_in(key_list[6], 71), 0),
        "intersection": draw_intersection(jax.random.fold_in(key_list[6], 71), 0),
        "offsets": draw_offsets(jax.random.fold_in(key_list[6], 71), 0),
        "science": draw_science(jax.random.fold_in(key_list[6], 71), 0),
        "weight": draw_weight(jax.random.fold_in(key_list[6], 71), 0),
        "positions": draw_positions(jax.random.fold_in(key_list[6], 71), 0),
    }


kernel_widths = (0.75, 1.5, 3.0)
poly_degrees = (4, 2, 2)
ridge_share = 0.02

def factor_taps(radius):
    tap_offsets = jnp.arange(-radius, radius + 1, dtype=jnp.float32)
    factor_rows = []
    for kernel_width, degree in zip(kernel_widths, poly_degrees):
        scaled = tap_offsets / kernel_width
        for exponent in range(degree + 1):
            values = scaled ** exponent * jnp.exp(-0.5 * scaled * scaled)
            factor_rows.append(values / jnp.sqrt(jnp.sum(values * values)))
    return jnp.stack(factor_rows).astype(jnp.float32)

def kernel_groups():
    groups = []
    first_slot = 0
    for kernel_width, degree in zip(kernel_widths, poly_degrees):
        for down_power in range(degree + 1):
            groups.append((first_slot + down_power, [first_slot + across_power for across_power in range(degree - down_power + 1)]))
        first_slot = first_slot + degree + 1
    return groups

def rounded(values):
    return lax.optimization_barrier(values.astype(jnp.bfloat16)).astype(jnp.float32)

def across_coord(quad_index, row_index):
    return (quad_index.astype(jnp.float32) * PIX + row_index.astype(jnp.float32) + 0.5) / (NQUAD * PIX) * 2.0 - 1.0

def side_coord(col_index):
    return (col_index.astype(jnp.float32) + 0.5) / PIX * 2.0 - 1.0

def horizontal_ref(window, tap_values):
    padded = jnp.pad(rounded(window), ((0, 0), (RADIUS, RADIUS)))
    running = jnp.zeros((tap_values.shape[0], PIX, PIX), jnp.float32)
    for tap_shift in range(2 * RADIUS + 1):
        running = running + tap_values[:, tap_shift][:, None, None] * padded[None, :, tap_shift:tap_shift + PIX]
    return rounded(running)

def vertical_ref(padded, tap_values, out_rows):
    image_parts = []
    for vertical, horizontals in kernel_groups():
        slab_rows = padded[horizontals[0]:horizontals[-1] + 1]
        running = jnp.zeros((len(horizontals), out_rows, padded.shape[2]), jnp.float32)
        for tap_shift in range(2 * RADIUS + 1):
            running = running + tap_values[vertical, tap_shift] * slab_rows[:, tap_shift:tap_shift + out_rows, :]
        image_parts.append(running)
    return jnp.concatenate(image_parts, 0)

def quad_normal(window, across_pass, science_quad, weight_quad, stamp_corners, quad_index, tap_values):
    padded = jnp.pad(across_pass, ((0, 0), (RADIUS, RADIUS), (0, 0)))
    stamp_range = jnp.arange(STAMP, dtype=jnp.int32)

    def stamp_terms(corner):
        stamp_top = corner[0].astype(jnp.int32)
        stamp_left = corner[1].astype(jnp.int32)
        slab_rows = lax.dynamic_slice(padded, (jnp.int32(0), stamp_top, stamp_left), (padded.shape[0], STAMP + 2 * RADIUS, STAMP))
        basis_images = vertical_ref(slab_rows, tap_values, STAMP)
        unit_image = jnp.ones((STAMP, STAMP), jnp.float32)
        features = jnp.concatenate([basis_images, unit_image[None]], 0)
        up_coord = across_coord(quad_index, stamp_top + stamp_range)
        right_coord = side_coord(stamp_left + stamp_range)
        spatial = jnp.stack([unit_image, up_coord[:, None] * unit_image, right_coord[None, :] * unit_image])
        design = (features[:, None] * spatial[None]).reshape(NCOEF, STAMP * STAMP)
        science_stamp = lax.dynamic_slice(science_quad, (stamp_top, stamp_left), (STAMP, STAMP)).reshape(-1)
        window_stamp = lax.dynamic_slice(window, (stamp_top, stamp_left), (STAMP, STAMP)).reshape(-1)
        weight_stamp = lax.dynamic_slice(weight_quad, (stamp_top, stamp_left), (STAMP, STAMP)).reshape(-1)
        weighted = design * weight_stamp[None]
        normal_matrix = jnp.dot(weighted.astype(jnp.float32), design.T.astype(jnp.float32), precision=lax.Precision.HIGHEST, preferred_element_type=jnp.float32)
        normal_vector = jnp.dot(weighted.astype(jnp.float32), (science_stamp - window_stamp).astype(jnp.float32), precision=lax.Precision.HIGHEST, preferred_element_type=jnp.float32)
        return (normal_matrix, normal_vector)
    matrices, vectors = jax.vmap(stamp_terms)(stamp_corners)
    return (lax.optimization_barrier(jnp.sum(matrices, 0)), lax.optimization_barrier(jnp.sum(vectors, 0)))

def solve_coefficients(normal_matrix, normal_vector):
    ridge_term = ridge_share * jnp.trace(normal_matrix) / NCOEF
    system = normal_matrix + ridge_term * jnp.eye(NCOEF, dtype=normal_matrix.dtype)
    factor_lower = jnp.linalg.cholesky(system)
    return jax.scipy.linalg.cho_solve((factor_lower, True), normal_vector)

def reference(template_patches, intersection, offsets, science, weight, positions):
    tap_values = rounded(factor_taps(RADIUS))
    quad_grid = jnp.broadcast_to(jnp.arange(NQUAD, dtype=jnp.int32)[None, :, None], intersection.shape)

    def one_band(patch_index, quad_index, first_row):
        return lax.dynamic_slice(template_patches, (patch_index.astype(jnp.int32), quad_index.astype(jnp.int32), first_row.astype(jnp.int32), jnp.int32(0)), (1, 1, BAND_ROWS, PIX))[0, 0]
    band_list = jax.vmap(one_band)(intersection.reshape(-1), quad_grid.reshape(-1), offsets.reshape(-1))
    windows = band_list.reshape(NCCD * NQUAD, PIX, PIX)
    quad_ids = jnp.tile(jnp.arange(NQUAD, dtype=jnp.int32), NCCD)
    science_flat = science.reshape(NCCD * NQUAD, PIX, PIX)
    weight_flat = weight.reshape(NCCD * NQUAD, PIX, PIX)
    corner_flat = positions.reshape(NCCD * NQUAD, NSTAMP, 2)

    def normal_one(quad_items):
        window, science_quad, weight_quad, stamp_corners, quad_index = quad_items
        across_pass = horizontal_ref(window, tap_values)
        return quad_normal(window, across_pass, science_quad, weight_quad, stamp_corners, quad_index, tap_values)
    matrices, vectors = lax.map(normal_one, (windows, science_flat, weight_flat, corner_flat, quad_ids))
    matrices = lax.optimization_barrier(jnp.sum(matrices.reshape(NCCD, NQUAD, NCOEF, NCOEF), 1))
    vectors = lax.optimization_barrier(jnp.sum(vectors.reshape(NCCD, NQUAD, NCOEF), 1))
    coefficients = jax.vmap(solve_coefficients)(matrices, vectors)
    quad_coefficients = jnp.repeat(coefficients, NQUAD, axis=0)
    pixel_range = jnp.arange(PIX, dtype=jnp.int32)

    def difference_one(quad_items):
        window, science_quad, quad_index, coeff_flat = quad_items
        across_pass = horizontal_ref(window, tap_values)
        padded = jnp.pad(across_pass, ((0, 0), (RADIUS, RADIUS), (0, 0)))
        basis_images = vertical_ref(padded, tap_values, PIX)
        coeff_table = coeff_flat.reshape(NBASIS + 1, 3)
        coeff_maps = jnp.einsum('ks,kyx->syx', coeff_table[:NBASIS], basis_images, precision=lax.Precision.HIGHEST)
        up_coord = across_coord(quad_index, pixel_range)[:, None]
        right_coord = side_coord(pixel_range)[None, :]
        model_image = coeff_maps[0] + up_coord * coeff_maps[1] + right_coord * coeff_maps[2]
        model_image = model_image + coeff_table[NBASIS, 0] + coeff_table[NBASIS, 1] * up_coord + coeff_table[NBASIS, 2] * right_coord
        return science_quad - window - model_image
    differences = lax.map(difference_one, (windows, science_flat, quad_ids, quad_coefficients))
    return differences.reshape(NCCD, NQUAD, PIX, PIX)
```

```python
import functools

import jax
import jax.numpy as jnp
import ml_dtypes
import numpy as np
from jax import lax
from jax.experimental import pallas as pl
from jax.experimental.pallas import tpu as pltpu
from jax.sharding import PartitionSpec as P

BANDS = 8
RADIUS = 10
NBASIS = 27
NCOEF = 84
STAMP = 32
NSTAMP = 32
NFACT = 11
TILE = 128
SLOT = 32
SLAB = 64
MARGIN = 16
ROWPAD = 64
GROUP = 4
CHUNK = 8
VMEM_LIMIT = 56 * 2**20

kernel_widths = (0.75, 1.5, 3.0)
poly_degrees = (4, 2, 2)
ridge_share = 0.02


def factor_taps():
    tap_offsets = np.arange(-RADIUS, RADIUS + 1, dtype=np.float64)
    factor_rows = []
    for kernel_width, degree in zip(kernel_widths, poly_degrees):
        scaled = tap_offsets / kernel_width
        for exponent in range(degree + 1):
            values = scaled**exponent * np.exp(-0.5 * scaled * scaled)
            factor_rows.append(values / np.sqrt(np.sum(values * values)))
    return np.stack(factor_rows).astype(np.float32).astype(ml_dtypes.bfloat16)


def kernel_list():
    pairs = []
    first_slot = 0
    for degree in poly_degrees:
        for down in range(degree + 1):
            for across in range(degree - down + 1):
                pairs.append((first_slot + down, first_slot + across))
        first_slot += degree + 1
    return pairs


PAIRS = kernel_list()
BY_ACROSS = [[k for k, (_, across) in enumerate(PAIRS) if across == f] for f in range(NFACT)]


def banded(taps, n_in, n_out, shift):
    offset = np.arange(n_in)[:, None] - shift - np.arange(n_out)[None, :]
    inside = np.abs(offset) <= RADIUS
    return np.where(inside, taps[np.clip(offset + RADIUS, 0, 2 * RADIUS)], 0)


@functools.lru_cache(None)
def tables():
    taps = factor_taps().astype(np.float32)
    across = np.concatenate([banded(t, 2 * TILE, TILE, ROWPAD) for t in taps], 1)
    stamp_across = np.zeros((GROUP * SLAB, NFACT * TILE), np.float32)
    for f in range(NFACT):
        block = banded(taps[f], SLAB, STAMP, MARGIN)
        for j in range(GROUP):
            stamp_across[
                j * SLAB : (j + 1) * SLAB, f * TILE + j * STAMP : f * TILE + (j + 1) * STAMP
            ] = block
    stamp_down = np.zeros((STAMP, SLOT, NFACT, SLAB), np.float32)
    for k, (down, f) in enumerate(PAIRS):
        stamp_down[:, k, f, :] = banded(taps[down], SLAB, STAMP, MARGIN).T
    stamp_down = stamp_down.reshape(STAMP * SLOT, NFACT * SLAB)
    down = np.concatenate(
        [banded(taps[PAIRS[k][0]], 2 * TILE, TILE, ROWPAD).T for ks in BY_ACROSS for k in ks], 0
    )
    return tuple(t.astype(ml_dtypes.bfloat16) for t in (across, stamp_across, stamp_down, down))


def rows_from(ref, first, count, lanes):
    start = jnp.minimum(lax.div(first, 8) * 8, ref.shape[0] - count - 8)
    start = pl.multiple_of(start, 8)
    value = ref[pl.ds(start, count + 8), lanes]
    turn = lax.rem(count + 8 - (first - start), count + 8)
    return pltpu.roll(value, turn, 0)[:count]


def greet(axis, count, me):
    barrier = pltpu.get_barrier_semaphore()
    for step in range(1, count):
        pl.semaphore_signal(
            barrier,
            inc=1,
            device_id={axis: lax.rem(me + step, count)},
            device_id_type=pl.DeviceIdType.MESH,
        )
    pl.semaphore_wait(barrier, count - 1)


def cut_kernel(count, band_rows, place, wanted, starts, patch, bands):
    for target in range(count):
        first = jnp.int32(0)
        for b in range(BANDS):
            first = first + jnp.where(wanted[target, b] == place[0], starts[target, b], 0)
        bands[target] = rows_from(patch, first, band_rows, slice(None))


def cut_bands(place, wanted, starts, patch, count):
    pixels = patch.shape[0]
    band_rows = pixels // BANDS
    vmem = pl.BlockSpec(memory_space=pltpu.VMEM)
    smem = pl.BlockSpec(memory_space=pltpu.SMEM)
    return pl.pallas_call(
        functools.partial(cut_kernel, count, band_rows),
        out_shape=jax.ShapeDtypeStruct((count, band_rows, pixels), jnp.float32),
        in_specs=[smem, smem, smem, vmem],
        out_specs=vmem,
        name="band_cut",
    )(place, wanted, starts, patch)


def exchange_kernel(count, bands, recv, send_sem, recv_sem, own_sem):
    me = lax.axis_index("ccd")
    own = pltpu.make_async_copy(bands.at[me], recv.at[me], own_sem)
    own.start()
    greet("ccd", count, me)
    copies = []
    for step in range(1, count):
        target = lax.rem(me + step, count)
        copy = pltpu.make_async_remote_copy(
            src_ref=bands.at[target],
            dst_ref=recv.at[me],
            send_sem=send_sem.at[step - 1],
            recv_sem=recv_sem.at[step - 1],
            device_id={"ccd": target},
            device_id_type=pl.DeviceIdType.MESH,
        )
        copy.start()
        copies.append(copy)
    for copy in copies:
        copy.wait()
    own.wait()


def exchange_bands(bands, count):
    return pl.pallas_call(
        functools.partial(exchange_kernel, count),
        out_shape=jax.ShapeDtypeStruct(bands.shape, jnp.float32),
        in_specs=[pl.BlockSpec(memory_space=pl.ANY)],
        out_specs=pl.BlockSpec(memory_space=pl.ANY),
        scratch_shapes=[
            pltpu.SemaphoreType.DMA((count - 1,)),
            pltpu.SemaphoreType.DMA((count - 1,)),
            pltpu.SemaphoreType.DMA,
        ],
        compiler_params=pltpu.CompilerParams(collective_id=0, has_side_effects=True),
        name="band_exchange",
    )(bands)


def normal_kernel(
    total_rows,
    place,
    wanted,
    corners,
    bands,
    science,
    weight,
    across_table,
    stamp_table,
    down_table,
    across,
    normal,
    rest,
    padded,
    shifted,
    slab_in,
    slab,
    root_weight,
    residual,
    up,
    side,
    halves,
):
    pixels = science.shape[0]
    band_rows = pixels // BANDS
    padded[...] = jnp.zeros_like(padded)
    for b in range(BANDS):
        rows = slice(b * band_rows, (b + 1) * band_rows)
        band = bands[wanted[place[0], b]]
        padded[MARGIN + b * band_rows : MARGIN + (b + 1) * band_rows, TILE : TILE + pixels] = band
        rest[rows, :] = science[rows, :] - band
    lane_slab = lax.broadcasted_iota(jnp.int32, (SLAB, GROUP * SLAB), 1) // SLAB
    lane_stamp = lax.broadcasted_iota(jnp.int32, (STAMP, TILE), 1) // STAMP
    lane_in = lax.broadcasted_iota(jnp.int32, (STAMP, TILE), 1) % STAMP
    row_in = lax.broadcasted_iota(jnp.int32, (STAMP, TILE), 0)

    for group in range(NSTAMP // GROUP):
        slab_value = jnp.zeros((SLAB, GROUP * SLAB), jnp.float32)
        rest_value = jnp.zeros((STAMP, TILE), jnp.float32)
        weight_value = jnp.zeros((STAMP, TILE), jnp.float32)
        row_of = jnp.zeros((STAMP, TILE), jnp.int32)
        col_of = jnp.zeros((STAMP, TILE), jnp.int32)
        for j in range(GROUP):
            top = corners[group * GROUP + j, 0]
            left = corners[group * GROUP + j, 1]
            first = left + (TILE - MARGIN)
            tile = pl.multiple_of(lax.div(first, TILE) * TILE, TILE)
            wide = rows_from(padded, top, SLAB, pl.ds(tile, 2 * TILE))
            wide = pltpu.roll(wide, lax.rem(j * SLAB - (first - tile) + 2 * TILE, 2 * TILE), 1)
            slab_value = jnp.where(lane_slab == j, wide, slab_value)
            tile = pl.multiple_of(lax.div(left, TILE) * TILE, TILE)
            turn = lax.rem(j * STAMP - (left - tile) + TILE, TILE)
            here = lane_stamp == j

            def cut(ref, before):
                piece = pltpu.roll(rows_from(ref, top, STAMP, pl.ds(tile, TILE)), turn, 1)
                return jnp.where(here, piece, before)

            rest_value = cut(rest, rest_value)
            weight_value = cut(weight, weight_value)
            row_of = jnp.where(here, top, row_of)
            col_of = jnp.where(here, left, col_of)
        slab_in[group * SLAB : (group + 1) * SLAB, :] = slab_value.astype(jnp.bfloat16)
        lanes = slice(group * TILE, (group + 1) * TILE)
        root_weight[:, lanes] = jnp.sqrt(weight_value)
        residual[:, lanes] = rest_value
        rows = (row_of + row_in + place[1] * pixels).astype(jnp.float32)
        up[:, lanes] = (rows + 0.5) / total_rows * 2.0 - 1.0
        columns = (col_of + lane_in).astype(jnp.float32)
        side[:, lanes] = (columns + 0.5) / pixels * 2.0 - 1.0

    groups = NSTAMP // GROUP
    for f in range(NFACT):
        part = jnp.dot(
            slab_in[...],
            stamp_table[:, f * TILE : (f + 1) * TILE],
            preferred_element_type=jnp.float32,
        ).astype(jnp.bfloat16)
        for group in range(groups):
            slab[f * SLAB : (f + 1) * SLAB, group * TILE : (group + 1) * TILE] = part[
                group * SLAB : (group + 1) * SLAB
            ]

    width = NSTAMP * STAMP
    feature = lax.broadcasted_iota(jnp.int32, (SLOT, width), 0)
    halves[...] = jnp.zeros_like(halves)

    def chunk_step(chunk, total):
        first = pl.multiple_of(chunk * (CHUNK * SLOT), CHUNK * SLOT)
        values = jnp.dot(
            down_table[pl.ds(first, CHUNK * SLOT), :],
            slab[...],
            preferred_element_type=jnp.float32,
        )
        row0 = pl.multiple_of(chunk * CHUNK, CHUNK)
        roots = root_weight[pl.ds(row0, CHUNK), :]
        rests = residual[pl.ds(row0, CHUNK), :]
        ups = up[pl.ds(row0, CHUNK), :]
        sides = side[pl.ds(row0, CHUNK), :]
        for a in range(CHUNK):
            lanes = slice(a * width, (a + 1) * width)
            basis = values[a * SLOT : (a + 1) * SLOT]
            basis = jnp.where(feature == NBASIS, 1.0, basis)
            basis = jnp.where(feature == NBASIS + 1, rests[a : a + 1], basis)
            basis = basis * roots[a : a + 1]
            for s, term in enumerate((basis, basis * ups[a : a + 1], basis * sides[a : a + 1])):
                high = term.astype(jnp.bfloat16)
                low = (term - high.astype(jnp.float32)).astype(jnp.bfloat16)
                halves[s * SLOT : (s + 1) * SLOT, lanes] = high
                halves[TILE + s * SLOT : TILE + (s + 1) * SLOT, lanes] = low
        return total + lax.dot_general(
            halves[0 : 3 * SLOT, :],
            halves[...],
            (((1,), (1,)), ((), ())),
            preferred_element_type=jnp.float32,
        )

    total = lax.fori_loop(
        0, STAMP // CHUNK, chunk_step, jnp.zeros((3 * SLOT, 2 * TILE), jnp.float32)
    )
    mixed = jnp.concatenate([total[:, TILE:], jnp.zeros((TILE - 3 * SLOT, TILE), jnp.float32)], 0)
    normal[...] = total[:, :TILE] + total[:, TILE:] + mixed.T[: 3 * SLOT]

    turned = pltpu.roll(padded[MARGIN : MARGIN + pixels, :], padded.shape[1] - ROWPAD, 1)
    shifted[...] = turned[:, : pixels + 2 * ROWPAD].astype(jnp.bfloat16)
    for f in range(NFACT):
        across[f, 0:ROWPAD, :] = jnp.zeros((ROWPAD, pixels), jnp.bfloat16)
        across[f, ROWPAD + pixels :, :] = jnp.zeros((ROWPAD, pixels), jnp.bfloat16)

    def across_step(tile, carry):
        first = pl.multiple_of(tile * TILE, TILE)
        source = shifted[:, pl.ds(first, 2 * TILE)]
        for f in range(NFACT):
            part = jnp.dot(
                source,
                across_table[:, f * TILE : (f + 1) * TILE],
                preferred_element_type=jnp.float32,
            )
            across[f, ROWPAD : ROWPAD + pixels, pl.ds(first, TILE)] = part.astype(jnp.bfloat16)
        return carry

    lax.fori_loop(0, pixels // TILE, across_step, 0)


def normal_equations(place, wanted, corners, bands, science, weight, total_rows):
    pixels = science.shape[0]
    across_table, stamp_table, down_table, _ = tables()
    width = NSTAMP * STAMP
    vmem = pl.BlockSpec(memory_space=pltpu.VMEM)
    smem = pl.BlockSpec(memory_space=pltpu.SMEM)
    return pl.pallas_call(
        functools.partial(normal_kernel, total_rows),
        out_shape=(
            jax.ShapeDtypeStruct((NFACT, pixels + 2 * ROWPAD, pixels), jnp.bfloat16),
            jax.ShapeDtypeStruct((3 * SLOT, TILE), jnp.float32),
            jax.ShapeDtypeStruct((pixels, pixels), jnp.float32),
        ),
        in_specs=[smem, smem, smem] + [vmem] * 6,
        out_specs=(vmem, vmem, vmem),
        scratch_shapes=[
            pltpu.VMEM((pixels + 3 * MARGIN, pixels + 2 * TILE), jnp.float32),
            pltpu.VMEM((pixels, pixels + 2 * ROWPAD), jnp.bfloat16),
            pltpu.VMEM((NSTAMP // GROUP * SLAB, GROUP * SLAB), jnp.bfloat16),
            pltpu.VMEM((NFACT * SLAB, width), jnp.bfloat16),
            pltpu.VMEM((STAMP, width), jnp.float32),
            pltpu.VMEM((STAMP, width), jnp.float32),
            pltpu.VMEM((STAMP, width), jnp.float32),
            pltpu.VMEM((STAMP, width), jnp.float32),
            pltpu.VMEM((2 * TILE, CHUNK * width), jnp.bfloat16),
        ],
        compiler_params=pltpu.CompilerParams(vmem_limit_bytes=VMEM_LIMIT),
        name="normal_equations",
    )(
        place,
        wanted,
        corners,
        bands,
        science,
        weight,
        jnp.asarray(across_table),
        jnp.asarray(stamp_table),
        jnp.asarray(down_table),
    )


def sum_kernel(count, part, total, recv, send_sem, recv_sem):
    me = lax.axis_index("quad")
    greet("quad", count, me)
    copies = []
    for step in range(1, count):
        copy = pltpu.make_async_remote_copy(
            src_ref=part,
            dst_ref=recv.at[step - 1],
            send_sem=send_sem.at[step - 1],
            recv_sem=recv_sem.at[step - 1],
            device_id={"quad": lax.rem(me + step, count)},
            device_id_type=pl.DeviceIdType.MESH,
        )
        copy.start()
        copies.append(copy)
    value = part[...]
    for step, copy in enumerate(copies):
        copy.wait()
        value = value + recv[step]
    total[...] = value


def sum_quadrants(part, count):
    vmem = pl.BlockSpec(memory_space=pltpu.VMEM)
    return pl.pallas_call(
        functools.partial(sum_kernel, count),
        out_shape=jax.ShapeDtypeStruct(part.shape, jnp.float32),
        in_specs=[vmem],
        out_specs=vmem,
        scratch_shapes=[
            pltpu.VMEM((count - 1,) + part.shape, jnp.float32),
            pltpu.SemaphoreType.DMA((count - 1,)),
            pltpu.SemaphoreType.DMA((count - 1,)),
        ],
        compiler_params=pltpu.CompilerParams(collective_id=1, has_side_effects=True),
        name="normal_sum",
    )(part)


def solve(normal):
    shape = normal.shape
    row = lax.broadcasted_iota(jnp.int32, shape, 0)
    lane = lax.broadcasted_iota(jnp.int32, shape, 1)
    row_used = row % SLOT <= NBASIS
    used = row_used & (lane % SLOT <= NBASIS) & (lane < 3 * SLOT)
    diagonal = row == lane
    trace = jnp.sum(jnp.where(used & diagonal, normal, 0.0))
    ridge = ridge_share * trace / NCOEF
    vector = jnp.sum(
        jnp.where((lane == NBASIS + 1) & row_used, normal, 0.0), axis=1, keepdims=True
    )
    system = jnp.where(used, normal, 0.0)
    system = system + jnp.where(diagonal, jnp.where(row_used, ridge, 1.0), 0.0)
    system = jnp.where(lane == 3 * SLOT, vector, system)
    for s in range(3):
        for k in range(NBASIS + 1):
            p = s * SLOT + k
            pivot_row = system[p : p + 1, :]
            pivot_row = pivot_row / pivot_row[:, p : p + 1]
            rest = system - system[:, p : p + 1] * pivot_row
            system = jnp.where(row == p, pivot_row, rest)
    return jnp.broadcast_to(system[:, 3 * SLOT : 3 * SLOT + 1], shape)


def difference_kernel(total_rows, place, normal, rest, across, table, out, coefficients, basis):
    pixels = rest.shape[0]
    coefficients[...] = solve(normal[...])
    tiles = pixels // TILE
    lane = lax.broadcasted_iota(jnp.int32, (8, pixels), 1).astype(jnp.float32)
    side = (lane + 0.5) / pixels * 2.0 - 1.0
    sub = lax.broadcasted_iota(jnp.int32, (8, TILE), 0)

    def tile_step(tile, carry):
        first = pl.multiple_of(tile * TILE, TILE)
        start = 0
        for f in range(NFACT):
            count = len(BY_ACROSS[f]) * TILE
            basis[start : start + count, :] = jnp.dot(
                table[start : start + count, :],
                across[f, pl.ds(first, 2 * TILE), :],
                preferred_element_type=jnp.float32,
            )
            start += count

        def row_step(chunk, inner):
            rows = pl.multiple_of(chunk * 8, 8)
            number = (place[1] * pixels + first + rows + sub).astype(jnp.float32)
            up = (number + 0.5) / total_rows * 2.0 - 1.0

            def terms(k):
                flat = coefficients[k : k + 1, :] + up * coefficients[SLOT + k : SLOT + k + 1, :]
                slope = jnp.broadcast_to(
                    coefficients[2 * SLOT + k : 2 * SLOT + k + 1, :], (8, TILE)
                )
                wide = pixels // TILE
                return jnp.concatenate([flat] * wide, 1), jnp.concatenate([slope] * wide, 1)

            flat_sum, slope_sum = terms(NBASIS)
            for index, k in enumerate([k for ks in BY_ACROSS for k in ks]):
                value = basis[pl.ds(index * TILE + rows, 8), :]
                flat, slope = terms(k)
                flat_sum = flat_sum + value * flat
                slope_sum = slope_sum + value * slope
            here = pl.ds(pl.multiple_of(first + rows, 8), 8)
            out[here, :] = rest[here, :] - (flat_sum + side * slope_sum)
            return inner

        lax.fori_loop(0, TILE // 8, row_step, 0)
        return carry

    lax.fori_loop(0, tiles, tile_step, 0)


def difference_image(place, normal, rest, across, total_rows):
    pixels = rest.shape[0]
    vmem = pl.BlockSpec(memory_space=pltpu.VMEM)
    smem = pl.BlockSpec(memory_space=pltpu.SMEM)
    return pl.pallas_call(
        functools.partial(difference_kernel, total_rows),
        out_shape=jax.ShapeDtypeStruct((pixels, pixels), jnp.float32),
        in_specs=[smem] + [vmem] * 4,
        out_specs=vmem,
        scratch_shapes=[
            pltpu.VMEM((3 * SLOT, TILE), jnp.float32),
            pltpu.VMEM((NBASIS * TILE, pixels), jnp.float32),
        ],
        compiler_params=pltpu.CompilerParams(vmem_limit_bytes=VMEM_LIMIT),
        name="difference",
    )(place, normal, rest, across, jnp.asarray(tables()[3]))


def local(template_patches, intersection, offsets, science, weight, positions):
    ccds = lax.axis_size("ccd")
    quads = lax.axis_size("quad")
    place = jnp.stack([lax.axis_index("ccd"), lax.axis_index("quad")]).astype(jnp.int32)
    pixels = science.shape[-1]
    total_rows = float(quads * pixels)
    wanted = intersection[:, 0]
    bands = cut_bands(place, wanted, offsets[:, 0], template_patches[0, 0], ccds)
    bands = exchange_bands(bands, ccds)
    across, normal, rest = normal_equations(
        place, wanted, positions[0, 0], bands, science[0, 0], weight[0, 0], total_rows
    )
    normal = sum_quadrants(normal, quads)
    image = difference_image(place, normal, rest, across, total_rows)
    return image[None, None]


def solution(mesh):
    return jax.shard_map(
        local,
        mesh=mesh,
        in_specs=(
            P("ccd", "quad", None, None),
            P(None, "quad", None),
            P(None, "quad", None),
            P("ccd", "quad", None, None),
            P("ccd", "quad", None, None),
            P("ccd", "quad", None, None),
        ),
        out_specs=P("ccd", "quad", None, None),
        check_vma=False,
    )
```

```python
import functools

import jax
import jax.numpy as jnp
import ml_dtypes
import numpy as np
from jax import lax
from jax.experimental import pallas as pl
from jax.experimental.pallas import tpu as pltpu
from jax.sharding import PartitionSpec as P

BANDS = 8
RADIUS = 10
NBASIS = 27
NCOEF = 84
STAMP = 32
NSTAMP = 32
NFACT = 11
TILE = 128
SLOT = 32
SLAB = 64
MARGIN = 16
ROWPAD = 64
GROUP = 4
CHUNK = 8
PIVOTS = 4
VMEM_LIMIT = 56 * 2**20

kernel_widths = (0.75, 1.5, 3.0)
poly_degrees = (4, 2, 2)
ridge_share = 0.02


def factor_taps():
    tap_offsets = np.arange(-RADIUS, RADIUS + 1, dtype=np.float64)
    factor_rows = []
    for kernel_width, degree in zip(kernel_widths, poly_degrees):
        scaled = tap_offsets / kernel_width
        for exponent in range(degree + 1):
            values = scaled**exponent * np.exp(-0.5 * scaled * scaled)
            factor_rows.append(values / np.sqrt(np.sum(values * values)))
    return np.stack(factor_rows).astype(np.float32).astype(ml_dtypes.bfloat16)


def kernel_list():
    pairs = []
    first_slot = 0
    for degree in poly_degrees:
        for down in range(degree + 1):
            for across in range(degree - down + 1):
                pairs.append((first_slot + down, first_slot + across))
        first_slot += degree + 1
    return pairs


PAIRS = kernel_list()
BY_ACROSS = [[k for k, (_, across) in enumerate(PAIRS) if across == f] for f in range(NFACT)]


def banded(taps, n_in, n_out, shift):
    offset = np.arange(n_in)[:, None] - shift - np.arange(n_out)[None, :]
    inside = np.abs(offset) <= RADIUS
    return np.where(inside, taps[np.clip(offset + RADIUS, 0, 2 * RADIUS)], 0)


@functools.lru_cache(None)
def tables():
    taps = factor_taps().astype(np.float32)
    across = np.concatenate([banded(t, 2 * TILE, TILE, ROWPAD) for t in taps], 1)
    stamp_across = np.zeros((GROUP * SLAB, NFACT * TILE), np.float32)
    for f in range(NFACT):
        block = banded(taps[f], SLAB, STAMP, MARGIN)
        for j in range(GROUP):
            stamp_across[
                j * SLAB : (j + 1) * SLAB, f * TILE + j * STAMP : f * TILE + (j + 1) * STAMP
            ] = block
    stamp_down = np.zeros((STAMP, SLOT, NFACT, SLAB), np.float32)
    for k, (down, f) in enumerate(PAIRS):
        stamp_down[:, k, f, :] = banded(taps[down], SLAB, STAMP, MARGIN).T
    stamp_down = stamp_down.reshape(STAMP * SLOT, NFACT * SLAB)
    down = np.concatenate(
        [banded(taps[PAIRS[k][0]], 2 * TILE, TILE, ROWPAD).T for ks in BY_ACROSS for k in ks], 0
    )
    return tuple(t.astype(ml_dtypes.bfloat16) for t in (across, stamp_across, stamp_down, down))


def rows_from(ref, first, count, lanes):
    start = jnp.minimum(lax.div(first, 8) * 8, ref.shape[0] - count - 8)
    start = pl.multiple_of(start, 8)
    value = ref[pl.ds(start, count + 8), lanes]
    turn = lax.rem(count + 8 - (first - start), count + 8)
    return pltpu.roll(value, turn, 0)[:count]


def greet(axis, count, me):
    barrier = pltpu.get_barrier_semaphore()
    for step in range(1, count):
        pl.semaphore_signal(
            barrier,
            inc=1,
            device_id={axis: lax.rem(me + step, count)},
            device_id_type=pl.DeviceIdType.MESH,
        )
    pl.semaphore_wait(barrier, count - 1)


def cut_kernel(count, band_rows, wanted, starts, patch, bands):
    me = lax.axis_index("ccd")
    for target in range(count):
        first = jnp.int32(0)
        for b in range(BANDS):
            first = first + jnp.where(wanted[target, b] == me, starts[target, b], 0)
        bands[target] = rows_from(patch, first, band_rows, slice(None))


def cut_bands(wanted, starts, patch, count):
    pixels = patch.shape[0]
    band_rows = pixels // BANDS
    vmem = pl.BlockSpec(memory_space=pltpu.VMEM)
    smem = pl.BlockSpec(memory_space=pltpu.SMEM)
    return pl.pallas_call(
        functools.partial(cut_kernel, count, band_rows),
        out_shape=jax.ShapeDtypeStruct((count, band_rows, pixels), jnp.float32),
        in_specs=[smem, smem, vmem],
        out_specs=vmem,
        name="band_cut",
    )(wanted, starts, patch)


def exchange_kernel(count, bands, recv, send_sem, recv_sem, own_sem):
    me = lax.axis_index("ccd")
    own = pltpu.make_async_copy(bands.at[me], recv.at[me], own_sem)
    own.start()
    greet("ccd", count, me)
    copies = []
    for step in range(1, count):
        target = lax.rem(me + step, count)
        copy = pltpu.make_async_remote_copy(
            src_ref=bands.at[target],
            dst_ref=recv.at[me],
            send_sem=send_sem.at[step - 1],
            recv_sem=recv_sem.at[step - 1],
            device_id={"ccd": target},
            device_id_type=pl.DeviceIdType.MESH,
        )
        copy.start()
        copies.append(copy)
    for copy in copies:
        copy.wait()
    own.wait()


def exchange_bands(bands, count):
    return pl.pallas_call(
        functools.partial(exchange_kernel, count),
        out_shape=jax.ShapeDtypeStruct(bands.shape, jnp.float32),
        in_specs=[pl.BlockSpec(memory_space=pl.ANY)],
        out_specs=pl.BlockSpec(memory_space=pl.ANY),
        scratch_shapes=[
            pltpu.SemaphoreType.DMA((count - 1,)),
            pltpu.SemaphoreType.DMA((count - 1,)),
            pltpu.SemaphoreType.DMA,
        ],
        compiler_params=pltpu.CompilerParams(collective_id=0, has_side_effects=True),
        name="band_exchange",
    )(bands)


def normal_kernel(
    total_rows,
    wanted,
    corners,
    bands,
    science,
    weight,
    stamp_table,
    down_table,
    shifted,
    normal,
    rest,
    padded,
    slab_in,
    slab,
    root_weight,
    residual,
    up,
    side,
    halves,
):
    pixels = science.shape[0]
    band_rows = pixels // BANDS
    me = lax.axis_index("ccd")
    quad = lax.axis_index("quad")
    padded[...] = jnp.zeros_like(padded)
    for b in range(BANDS):
        rows = slice(b * band_rows, (b + 1) * band_rows)
        band = bands[wanted[me, b]]
        padded[MARGIN + b * band_rows : MARGIN + (b + 1) * band_rows, TILE : TILE + pixels] = band
        rest[rows, :] = science[rows, :] - band
    lane_slab = lax.broadcasted_iota(jnp.int32, (SLAB, GROUP * SLAB), 1) // SLAB
    lane_stamp = lax.broadcasted_iota(jnp.int32, (STAMP, TILE), 1) // STAMP
    lane_in = lax.broadcasted_iota(jnp.int32, (STAMP, TILE), 1) % STAMP
    row_in = lax.broadcasted_iota(jnp.int32, (STAMP, TILE), 0)

    for group in range(NSTAMP // GROUP):
        slab_value = jnp.zeros((SLAB, GROUP * SLAB), jnp.float32)
        rest_value = jnp.zeros((STAMP, TILE), jnp.float32)
        weight_value = jnp.zeros((STAMP, TILE), jnp.float32)
        row_of = jnp.zeros((STAMP, TILE), jnp.int32)
        col_of = jnp.zeros((STAMP, TILE), jnp.int32)
        for j in range(GROUP):
            top = corners[0, group * GROUP + j]
            left = corners[1, group * GROUP + j]
            first = left + (TILE - MARGIN)
            tile = pl.multiple_of(lax.div(first, TILE) * TILE, TILE)
            wide = rows_from(padded, top, SLAB, pl.ds(tile, 2 * TILE))
            wide = pltpu.roll(wide, lax.rem(j * SLAB - (first - tile) + 2 * TILE, 2 * TILE), 1)
            slab_value = jnp.where(lane_slab == j, wide, slab_value)
            tile = pl.multiple_of(lax.div(left, TILE) * TILE, TILE)
            turn = lax.rem(j * STAMP - (left - tile) + TILE, TILE)
            here = lane_stamp == j

            def cut(ref, before):
                piece = pltpu.roll(rows_from(ref, top, STAMP, pl.ds(tile, TILE)), turn, 1)
                return jnp.where(here, piece, before)

            rest_value = cut(rest, rest_value)
            weight_value = cut(weight, weight_value)
            row_of = jnp.where(here, top, row_of)
            col_of = jnp.where(here, left, col_of)
        slab_in[group * SLAB : (group + 1) * SLAB, :] = slab_value.astype(jnp.bfloat16)
        lanes = slice(group * TILE, (group + 1) * TILE)
        root_weight[:, lanes] = jnp.sqrt(weight_value)
        residual[:, lanes] = rest_value
        rows = (row_of + row_in + quad * pixels).astype(jnp.float32)
        up[:, lanes] = (rows + 0.5) / total_rows * 2.0 - 1.0
        columns = (col_of + lane_in).astype(jnp.float32)
        side[:, lanes] = (columns + 0.5) / pixels * 2.0 - 1.0

    groups = NSTAMP // GROUP
    for f in range(NFACT):
        part = jnp.dot(
            slab_in[...],
            stamp_table[:, f * TILE : (f + 1) * TILE],
            preferred_element_type=jnp.float32,
        ).astype(jnp.bfloat16)
        for group in range(groups):
            slab[f * SLAB : (f + 1) * SLAB, group * TILE : (group + 1) * TILE] = part[
                group * SLAB : (group + 1) * SLAB
            ]

    width = NSTAMP * STAMP
    feature = lax.broadcasted_iota(jnp.int32, (SLOT, width), 0)
    halves[...] = jnp.zeros_like(halves)

    def chunk_step(chunk, total):
        first = pl.multiple_of(chunk * (CHUNK * SLOT), CHUNK * SLOT)
        values = jnp.dot(
            down_table[pl.ds(first, CHUNK * SLOT), :],
            slab[...],
            preferred_element_type=jnp.float32,
        )
        row0 = pl.multiple_of(chunk * CHUNK, CHUNK)
        roots = root_weight[pl.ds(row0, CHUNK), :]
        rests = residual[pl.ds(row0, CHUNK), :]
        ups = up[pl.ds(row0, CHUNK), :]
        sides = side[pl.ds(row0, CHUNK), :]
        for a in range(CHUNK):
            lanes = slice(a * width, (a + 1) * width)
            basis = values[a * SLOT : (a + 1) * SLOT]
            basis = jnp.where(feature == NBASIS, 1.0, basis)
            basis = jnp.where(feature == NBASIS + 1, rests[a : a + 1], basis)
            basis = basis * roots[a : a + 1]
            for s, term in enumerate((basis, basis * ups[a : a + 1], basis * sides[a : a + 1])):
                high = term.astype(jnp.bfloat16)
                low = (term - high.astype(jnp.float32)).astype(jnp.bfloat16)
                halves[s * SLOT : (s + 1) * SLOT, lanes] = high
                halves[TILE + s * SLOT : TILE + (s + 1) * SLOT, lanes] = low
        return total + lax.dot_general(
            halves[0 : 3 * SLOT, :],
            halves[...],
            (((1,), (1,)), ((), ())),
            preferred_element_type=jnp.float32,
        )

    total = lax.fori_loop(
        0, STAMP // CHUNK, chunk_step, jnp.zeros((3 * SLOT, 2 * TILE), jnp.float32)
    )
    mixed = jnp.concatenate([total[:, TILE:], jnp.zeros((TILE - 3 * SLOT, TILE), jnp.float32)], 0)
    normal[...] = total[:, :TILE] + total[:, TILE:] + mixed.T[: 3 * SLOT]

    turned = pltpu.roll(padded[MARGIN : MARGIN + pixels, :], padded.shape[1] - ROWPAD, 1)
    shifted[...] = turned[:, : pixels + 2 * ROWPAD].astype(jnp.bfloat16)


def normal_equations(wanted, corners, bands, science, weight, total_rows):
    pixels = science.shape[0]
    _, stamp_table, down_table, _ = tables()
    width = NSTAMP * STAMP
    vmem = pl.BlockSpec(memory_space=pltpu.VMEM)
    smem = pl.BlockSpec(memory_space=pltpu.SMEM)
    return pl.pallas_call(
        functools.partial(normal_kernel, total_rows),
        out_shape=(
            jax.ShapeDtypeStruct((pixels, pixels + 2 * ROWPAD), jnp.bfloat16),
            jax.ShapeDtypeStruct((3 * SLOT, TILE), jnp.float32),
            jax.ShapeDtypeStruct((pixels, pixels), jnp.float32),
        ),
        in_specs=[smem, smem] + [vmem] * 5,
        out_specs=(vmem, vmem, vmem),
        scratch_shapes=[
            pltpu.VMEM((pixels + 3 * MARGIN, pixels + 2 * TILE), jnp.float32),
            pltpu.VMEM((NSTAMP // GROUP * SLAB, GROUP * SLAB), jnp.bfloat16),
            pltpu.VMEM((NFACT * SLAB, width), jnp.bfloat16),
            pltpu.VMEM((STAMP, width), jnp.float32),
            pltpu.VMEM((STAMP, width), jnp.float32),
            pltpu.VMEM((STAMP, width), jnp.float32),
            pltpu.VMEM((STAMP, width), jnp.float32),
            pltpu.VMEM((2 * TILE, CHUNK * width), jnp.bfloat16),
        ],
        compiler_params=pltpu.CompilerParams(vmem_limit_bytes=VMEM_LIMIT),
        name="normal_equations",
    )(
        wanted,
        corners,
        bands,
        science,
        weight,
        jnp.asarray(stamp_table),
        jnp.asarray(down_table),
    )


def solve(normal):
    shape = normal.shape
    row = lax.broadcasted_iota(jnp.int32, shape, 0)
    lane = lax.broadcasted_iota(jnp.int32, shape, 1)
    row_used = row % SLOT <= NBASIS
    used = row_used & (lane % SLOT <= NBASIS) & (lane < 3 * SLOT)
    diagonal = row == lane
    trace = jnp.sum(jnp.where(used & diagonal, normal, 0.0))
    ridge = ridge_share * trace / NCOEF
    vector = jnp.sum(
        jnp.where((lane == NBASIS + 1) & row_used, normal, 0.0), axis=1, keepdims=True
    )
    system = jnp.where(used, normal, 0.0)
    system = system + jnp.where(diagonal, jnp.where(row_used, ridge, 1.0), 0.0)
    system = jnp.where(lane == 3 * SLOT, vector, system)
    for block in range(NCOEF // PIVOTS):
        per_term = (NBASIS + 1) // PIVOTS
        p = block // per_term * SLOT + block % per_term * PIVOTS
        span = range(PIVOTS)
        columns = [jnp.broadcast_to(system[:, p + j : p + j + 1], shape) for j in span]
        rows = [system[p + i : p + i + 1, :] for i in span]
        entry = [[columns[j][p + i : p + i + 1, :] for j in span] for i in span]
        for i in span:
            inverse = 1.0 / entry[i][i]
            rows[i] = rows[i] * inverse
            for j in range(i + 1, PIVOTS):
                entry[i][j] = entry[i][j] * inverse
            for m in span:
                if m != i:
                    rows[m] = rows[m] - entry[m][i] * rows[i]
                    for j in range(i + 1, PIVOTS):
                        entry[m][j] = entry[m][j] - entry[m][i] * entry[i][j]
        for j in span:
            system = system - columns[j] * rows[j]
        for i in span:
            system = jnp.where(row == p + i, rows[i], system)
    return jnp.broadcast_to(system[:, 3 * SLOT : 3 * SLOT + 1], shape)


def difference_kernel(
    count,
    part,
    shifted,
    rest,
    across_table,
    table,
    out,
    across,
    coefficients,
    basis,
    recv,
    send_sem,
    recv_sem,
):
    pixels = rest.shape[0]
    total_rows = float(count * pixels)
    me = lax.axis_index("quad")
    greet("quad", count, me)
    copies = []
    for step in range(1, count):
        copy = pltpu.make_async_remote_copy(
            src_ref=part,
            dst_ref=recv.at[step - 1],
            send_sem=send_sem.at[step - 1],
            recv_sem=recv_sem.at[step - 1],
            device_id={"quad": lax.rem(me + step, count)},
            device_id_type=pl.DeviceIdType.MESH,
        )
        copy.start()
        copies.append(copy)

    for f in range(NFACT):
        across[f, 0:ROWPAD, :] = jnp.zeros((ROWPAD, pixels), jnp.bfloat16)
        across[f, ROWPAD + pixels :, :] = jnp.zeros((ROWPAD, pixels), jnp.bfloat16)

    def across_step(tile, carry):
        first = pl.multiple_of(tile * TILE, TILE)
        source = shifted[:, pl.ds(first, 2 * TILE)]
        for f in range(NFACT):
            value = jnp.dot(
                source,
                across_table[:, f * TILE : (f + 1) * TILE],
                preferred_element_type=jnp.float32,
            )
            across[f, ROWPAD : ROWPAD + pixels, pl.ds(first, TILE)] = value.astype(jnp.bfloat16)
        return carry

    lax.fori_loop(0, pixels // TILE, across_step, 0)

    normal = part[...]
    for step, copy in enumerate(copies):
        copy.wait()
        normal = normal + recv[step]
    coefficients[...] = solve(normal)
    tiles = pixels // TILE
    lane = lax.broadcasted_iota(jnp.int32, (8, pixels), 1).astype(jnp.float32)
    side = (lane + 0.5) / pixels * 2.0 - 1.0
    sub = lax.broadcasted_iota(jnp.int32, (8, TILE), 0)

    def tile_step(tile, carry):
        first = pl.multiple_of(tile * TILE, TILE)
        start = 0
        for f in range(NFACT):
            count = len(BY_ACROSS[f]) * TILE
            basis[start : start + count, :] = jnp.dot(
                table[start : start + count, :],
                across[f, pl.ds(first, 2 * TILE), :],
                preferred_element_type=jnp.float32,
            )
            start += count

        def row_step(chunk, inner):
            rows = pl.multiple_of(chunk * 8, 8)
            number = (me * pixels + first + rows + sub).astype(jnp.float32)
            up = (number + 0.5) / total_rows * 2.0 - 1.0

            def terms(k):
                flat = coefficients[k : k + 1, :] + up * coefficients[SLOT + k : SLOT + k + 1, :]
                slope = jnp.broadcast_to(
                    coefficients[2 * SLOT + k : 2 * SLOT + k + 1, :], (8, TILE)
                )
                wide = pixels // TILE
                return jnp.concatenate([flat] * wide, 1), jnp.concatenate([slope] * wide, 1)

            flat_sum, slope_sum = terms(NBASIS)
            for index, k in enumerate([k for ks in BY_ACROSS for k in ks]):
                value = basis[pl.ds(index * TILE + rows, 8), :]
                flat, slope = terms(k)
                flat_sum = flat_sum + value * flat
                slope_sum = slope_sum + value * slope
            here = pl.ds(pl.multiple_of(first + rows, 8), 8)
            out[here, :] = rest[here, :] - (flat_sum + side * slope_sum)
            return inner

        lax.fori_loop(0, TILE // 8, row_step, 0)
        return carry

    lax.fori_loop(0, tiles, tile_step, 0)


def difference_image(part, shifted, rest, count):
    pixels = rest.shape[0]
    vmem = pl.BlockSpec(memory_space=pltpu.VMEM)
    across_table, _, _, table = tables()
    return pl.pallas_call(
        functools.partial(difference_kernel, count),
        out_shape=jax.ShapeDtypeStruct((pixels, pixels), jnp.float32),
        in_specs=[vmem] * 5,
        out_specs=vmem,
        scratch_shapes=[
            pltpu.VMEM((NFACT, pixels + 2 * ROWPAD, pixels), jnp.bfloat16),
            pltpu.VMEM((3 * SLOT, TILE), jnp.float32),
            pltpu.VMEM((NBASIS * TILE, pixels), jnp.float32),
            pltpu.VMEM((count - 1,) + part.shape, jnp.float32),
            pltpu.SemaphoreType.DMA((count - 1,)),
            pltpu.SemaphoreType.DMA((count - 1,)),
        ],
        compiler_params=pltpu.CompilerParams(
            collective_id=1, has_side_effects=True, vmem_limit_bytes=VMEM_LIMIT
        ),
        name="difference",
    )(part, shifted, rest, jnp.asarray(across_table), jnp.asarray(table))


def local(template_patches, intersection, offsets, science, weight, positions):
    ccds = lax.axis_size("ccd")
    quads = lax.axis_size("quad")
    pixels = science.shape[-1]
    total_rows = float(quads * pixels)
    wanted = intersection[:, 0]
    bands = cut_bands(wanted, offsets[:, 0], template_patches[0, 0], ccds)
    bands = exchange_bands(bands, ccds)
    shifted, normal, rest = normal_equations(
        wanted, positions[0, 0].T, bands, science[0, 0], weight[0, 0], total_rows
    )
    image = difference_image(normal, shifted, rest, quads)
    return image[None, None]


def solution(mesh):
    return jax.shard_map(
        local,
        mesh=mesh,
        in_specs=(
            P("ccd", "quad", None, None),
            P(None, "quad", None),
            P(None, "quad", None),
            P("ccd", "quad", None, None),
            P("ccd", "quad", None, None),
            P("ccd", "quad", None, None),
        ),
        out_specs=P("ccd", "quad", None, None),
        check_vma=False,
    )
```

```python
import functools

import jax
import jax.numpy as jnp
import ml_dtypes
import numpy as np
from jax import lax
from jax.experimental import pallas as pl
from jax.experimental.pallas import tpu as pltpu
from jax.sharding import PartitionSpec as P

BANDS = 8
RADIUS = 10
NBASIS = 27
NCOEF = 84
STAMP = 32
NSTAMP = 32
NFACT = 11
TILE = 128
SLOT = 32
SLAB = 64
MARGIN = 16
ROWPAD = 64
GROUP = 4
CHUNK = 8
PIVOTS = 4
NORMAL_VMEM = 24 * 2**20
DIFFERENCE_VMEM = 30 * 2**20

kernel_widths = (0.75, 1.5, 3.0)
poly_degrees = (4, 2, 2)
ridge_share = 0.02


def factor_taps():
    tap_offsets = np.arange(-RADIUS, RADIUS + 1, dtype=np.float64)
    factor_rows = []
    for kernel_width, degree in zip(kernel_widths, poly_degrees):
        scaled = tap_offsets / kernel_width
        for exponent in range(degree + 1):
            values = scaled**exponent * np.exp(-0.5 * scaled * scaled)
            factor_rows.append(values / np.sqrt(np.sum(values * values)))
    return np.stack(factor_rows).astype(np.float32).astype(ml_dtypes.bfloat16)


def kernel_list():
    pairs = []
    first_slot = 0
    for degree in poly_degrees:
        for down in range(degree + 1):
            for across in range(degree - down + 1):
                pairs.append((first_slot + down, first_slot + across))
        first_slot += degree + 1
    return pairs


PAIRS = kernel_list()
BY_ACROSS = [[k for k, (_, across) in enumerate(PAIRS) if across == f] for f in range(NFACT)]


def banded(taps, n_in, n_out, shift):
    offset = np.arange(n_in)[:, None] - shift - np.arange(n_out)[None, :]
    inside = np.abs(offset) <= RADIUS
    return np.where(inside, taps[np.clip(offset + RADIUS, 0, 2 * RADIUS)], 0)


@functools.lru_cache(None)
def tables():
    taps = factor_taps().astype(np.float32)
    across = np.concatenate([banded(t, 2 * TILE, TILE, ROWPAD) for t in taps], 1)
    stamp_across = np.zeros((GROUP * SLAB, NFACT * TILE), np.float32)
    for f in range(NFACT):
        block = banded(taps[f], SLAB, STAMP, MARGIN)
        for j in range(GROUP):
            stamp_across[
                j * SLAB : (j + 1) * SLAB, f * TILE + j * STAMP : f * TILE + (j + 1) * STAMP
            ] = block
    stamp_down = np.zeros((STAMP, SLOT, NFACT, SLAB), np.float32)
    for k, (down, f) in enumerate(PAIRS):
        stamp_down[:, k, f, :] = banded(taps[down], SLAB, STAMP, MARGIN).T
    stamp_down = stamp_down.reshape(STAMP * SLOT, NFACT * SLAB)
    down = np.concatenate(
        [banded(taps[PAIRS[k][0]], 2 * TILE, TILE, ROWPAD).T for ks in BY_ACROSS for k in ks], 0
    )
    return tuple(t.astype(ml_dtypes.bfloat16) for t in (across, stamp_across, stamp_down, down))


def rows_from(ref, first, count, lanes):
    start = jnp.minimum(lax.div(first, 8) * 8, ref.shape[0] - count - 8)
    start = pl.multiple_of(start, 8)
    value = ref[pl.ds(start, count + 8), lanes]
    turn = lax.rem(count + 8 - (first - start), count + 8)
    return pltpu.roll(value, turn, 0)[:count]


def greet(axis, count, me):
    barrier = pltpu.get_barrier_semaphore()
    for step in range(1, count):
        pl.semaphore_signal(
            barrier,
            inc=1,
            device_id={axis: lax.rem(me + step, count)},
            device_id_type=pl.DeviceIdType.MESH,
        )
    pl.semaphore_wait(barrier, count - 1)


def cut_kernel(count, band_rows, wanted, starts, patch, bands):
    me = lax.axis_index("ccd")
    for target in range(count):
        first = jnp.int32(0)
        for b in range(BANDS):
            first = first + jnp.where(wanted[target, b] == me, starts[target, b], 0)
        bands[target] = rows_from(patch, first, band_rows, slice(None))


def cut_bands(wanted, starts, patch, count):
    pixels = patch.shape[0]
    band_rows = pixels // BANDS
    vmem = pl.BlockSpec(memory_space=pltpu.VMEM)
    smem = pl.BlockSpec(memory_space=pltpu.SMEM)
    return pl.pallas_call(
        functools.partial(cut_kernel, count, band_rows),
        out_shape=jax.ShapeDtypeStruct((count, band_rows, pixels), jnp.float32),
        in_specs=[smem, smem, vmem],
        out_specs=vmem,
        name="band_cut",
    )(wanted, starts, patch)


def exchange_kernel(count, bands, recv, send_sem, recv_sem, own_sem):
    me = lax.axis_index("ccd")
    own = pltpu.make_async_copy(bands.at[me], recv.at[me], own_sem)
    own.start()
    greet("ccd", count, me)
    copies = []
    for step in range(1, count):
        target = lax.rem(me + step, count)
        copy = pltpu.make_async_remote_copy(
            src_ref=bands.at[target],
            dst_ref=recv.at[me],
            send_sem=send_sem.at[step - 1],
            recv_sem=recv_sem.at[step - 1],
            device_id={"ccd": target},
            device_id_type=pl.DeviceIdType.MESH,
        )
        copy.start()
        copies.append(copy)
    for copy in copies:
        copy.wait()
    own.wait()


def exchange_bands(bands, count):
    return pl.pallas_call(
        functools.partial(exchange_kernel, count),
        out_shape=jax.ShapeDtypeStruct(bands.shape, jnp.float32),
        in_specs=[pl.BlockSpec(memory_space=pl.ANY)],
        out_specs=pl.BlockSpec(memory_space=pl.ANY),
        scratch_shapes=[
            pltpu.SemaphoreType.DMA((count - 1,)),
            pltpu.SemaphoreType.DMA((count - 1,)),
            pltpu.SemaphoreType.DMA,
        ],
        compiler_params=pltpu.CompilerParams(collective_id=0, has_side_effects=True),
        name="band_exchange",
    )(bands)


def normal_kernel(
    total_rows,
    wanted,
    corners,
    bands,
    science,
    weight,
    stamp_table,
    down_table,
    shifted,
    normal,
    rest,
    padded,
    slab_in,
    slab,
    root_weight,
    residual,
    up,
    side,
    halves,
):
    pixels = science.shape[0]
    band_rows = pixels // BANDS
    me = lax.axis_index("ccd")
    quad = lax.axis_index("quad")
    padded[...] = jnp.zeros_like(padded)
    for b in range(BANDS):
        rows = slice(b * band_rows, (b + 1) * band_rows)
        band = bands[wanted[me, b]]
        padded[MARGIN + b * band_rows : MARGIN + (b + 1) * band_rows, TILE : TILE + pixels] = band
        rest[rows, :] = science[rows, :] - band
    lane_slab = lax.broadcasted_iota(jnp.int32, (SLAB, GROUP * SLAB), 1) // SLAB
    lane_stamp = lax.broadcasted_iota(jnp.int32, (STAMP, TILE), 1) // STAMP
    lane_in = lax.broadcasted_iota(jnp.int32, (STAMP, TILE), 1) % STAMP
    row_in = lax.broadcasted_iota(jnp.int32, (STAMP, TILE), 0)

    for group in range(NSTAMP // GROUP):
        slab_value = jnp.zeros((SLAB, GROUP * SLAB), jnp.float32)
        rest_value = jnp.zeros((STAMP, TILE), jnp.float32)
        weight_value = jnp.zeros((STAMP, TILE), jnp.float32)
        row_of = jnp.zeros((STAMP, TILE), jnp.int32)
        col_of = jnp.zeros((STAMP, TILE), jnp.int32)
        for j in range(GROUP):
            top = corners[0, group * GROUP + j]
            left = corners[1, group * GROUP + j]
            first = left + (TILE - MARGIN)
            tile = pl.multiple_of(lax.div(first, TILE) * TILE, TILE)
            wide = rows_from(padded, top, SLAB, pl.ds(tile, 2 * TILE))
            wide = pltpu.roll(wide, lax.rem(j * SLAB - (first - tile) + 2 * TILE, 2 * TILE), 1)
            slab_value = jnp.where(lane_slab == j, wide, slab_value)
            tile = pl.multiple_of(lax.div(left, TILE) * TILE, TILE)
            turn = lax.rem(j * STAMP - (left - tile) + TILE, TILE)
            here = lane_stamp == j

            def cut(ref, before):
                piece = pltpu.roll(rows_from(ref, top, STAMP, pl.ds(tile, TILE)), turn, 1)
                return jnp.where(here, piece, before)

            rest_value = cut(rest, rest_value)
            weight_value = cut(weight, weight_value)
            row_of = jnp.where(here, top, row_of)
            col_of = jnp.where(here, left, col_of)
        slab_in[group * SLAB : (group + 1) * SLAB, :] = slab_value.astype(jnp.bfloat16)
        lanes = slice(group * TILE, (group + 1) * TILE)
        root_weight[:, lanes] = jnp.sqrt(weight_value)
        residual[:, lanes] = rest_value
        rows = (row_of + row_in + quad * pixels).astype(jnp.float32)
        up[:, lanes] = (rows + 0.5) / total_rows * 2.0 - 1.0
        columns = (col_of + lane_in).astype(jnp.float32)
        side[:, lanes] = (columns + 0.5) / pixels * 2.0 - 1.0

    groups = NSTAMP // GROUP
    for pair in range(0, NFACT, 2):
        last = min(pair + 2, NFACT)
        part = jnp.dot(
            slab_in[...],
            stamp_table[:, pair * TILE : last * TILE],
            preferred_element_type=jnp.float32,
        ).astype(jnp.bfloat16)
        for f in range(pair, last):
            for group in range(groups):
                slab[f * SLAB : (f + 1) * SLAB, group * TILE : (group + 1) * TILE] = part[
                    group * SLAB : (group + 1) * SLAB, (f - pair) * TILE : (f - pair + 1) * TILE
                ]

    width = NSTAMP * STAMP
    feature = lax.broadcasted_iota(jnp.int32, (SLOT, width), 0)
    halves[...] = jnp.zeros_like(halves)

    def chunk_step(chunk, total):
        first = pl.multiple_of(chunk * (CHUNK * SLOT), CHUNK * SLOT)
        values = jnp.dot(
            down_table[pl.ds(first, CHUNK * SLOT), :],
            slab[...],
            preferred_element_type=jnp.float32,
        )
        row0 = pl.multiple_of(chunk * CHUNK, CHUNK)
        roots = root_weight[pl.ds(row0, CHUNK), :]
        rests = residual[pl.ds(row0, CHUNK), :]
        ups = up[pl.ds(row0, CHUNK), :]
        sides = side[pl.ds(row0, CHUNK), :]
        for a in range(CHUNK):
            lanes = slice(a * width, (a + 1) * width)
            basis = values[a * SLOT : (a + 1) * SLOT]
            basis = jnp.where(feature == NBASIS, 1.0, basis)
            basis = jnp.where(feature == NBASIS + 1, rests[a : a + 1], basis)
            basis = basis * roots[a : a + 1]
            for s, term in enumerate((basis, basis * ups[a : a + 1], basis * sides[a : a + 1])):
                high = term.astype(jnp.bfloat16)
                low = (term - high.astype(jnp.float32)).astype(jnp.bfloat16)
                halves[s * SLOT : (s + 1) * SLOT, lanes] = high
                halves[TILE + s * SLOT : TILE + (s + 1) * SLOT, lanes] = low
        return total + lax.dot_general(
            halves[0 : 3 * SLOT, :],
            halves[...],
            (((1,), (1,)), ((), ())),
            preferred_element_type=jnp.float32,
        )

    total = lax.fori_loop(
        0, STAMP // CHUNK, chunk_step, jnp.zeros((3 * SLOT, 2 * TILE), jnp.float32)
    )
    mixed = jnp.concatenate([total[:, TILE:], jnp.zeros((TILE - 3 * SLOT, TILE), jnp.float32)], 0)
    normal[...] = total[:, :TILE] + total[:, TILE:] + mixed.T[: 3 * SLOT]

    turned = pltpu.roll(padded[MARGIN : MARGIN + pixels, :], padded.shape[1] - ROWPAD, 1)
    shifted[...] = turned[:, : pixels + 2 * ROWPAD].astype(jnp.bfloat16)


def normal_equations(wanted, corners, bands, science, weight, total_rows):
    pixels = science.shape[0]
    _, stamp_table, down_table, _ = tables()
    width = NSTAMP * STAMP
    vmem = pl.BlockSpec(memory_space=pltpu.VMEM)
    smem = pl.BlockSpec(memory_space=pltpu.SMEM)
    return pl.pallas_call(
        functools.partial(normal_kernel, total_rows),
        out_shape=(
            jax.ShapeDtypeStruct((pixels, pixels + 2 * ROWPAD), jnp.bfloat16),
            jax.ShapeDtypeStruct((3 * SLOT, TILE), jnp.float32),
            jax.ShapeDtypeStruct((pixels, pixels), jnp.float32),
        ),
        in_specs=[smem, smem] + [vmem] * 5,
        out_specs=(vmem, vmem, vmem),
        scratch_shapes=[
            pltpu.VMEM((pixels + 3 * MARGIN, pixels + 2 * TILE), jnp.float32),
            pltpu.VMEM((NSTAMP // GROUP * SLAB, GROUP * SLAB), jnp.bfloat16),
            pltpu.VMEM((NFACT * SLAB, width), jnp.bfloat16),
            pltpu.VMEM((STAMP, width), jnp.float32),
            pltpu.VMEM((STAMP, width), jnp.float32),
            pltpu.VMEM((STAMP, width), jnp.float32),
            pltpu.VMEM((STAMP, width), jnp.float32),
            pltpu.VMEM((2 * TILE, CHUNK * width), jnp.bfloat16),
        ],
        compiler_params=pltpu.CompilerParams(vmem_limit_bytes=NORMAL_VMEM),
        name="normal_equations",
    )(
        wanted,
        corners,
        bands,
        science,
        weight,
        jnp.asarray(stamp_table),
        jnp.asarray(down_table),
    )


def solve(normal):
    shape = normal.shape
    row = lax.broadcasted_iota(jnp.int32, shape, 0)
    lane = lax.broadcasted_iota(jnp.int32, shape, 1)
    row_used = row % SLOT <= NBASIS
    used = row_used & (lane % SLOT <= NBASIS) & (lane < 3 * SLOT)
    diagonal = row == lane
    trace = jnp.sum(jnp.where(used & diagonal, normal, 0.0))
    ridge = ridge_share * trace / NCOEF
    vector = jnp.sum(
        jnp.where((lane == NBASIS + 1) & row_used, normal, 0.0), axis=1, keepdims=True
    )
    system = jnp.where(used, normal, 0.0)
    system = system + jnp.where(diagonal, jnp.where(row_used, ridge, 1.0), 0.0)
    system = jnp.where(lane == 3 * SLOT, vector, system)
    for block in range(NCOEF // PIVOTS):
        per_term = (NBASIS + 1) // PIVOTS
        p = block // per_term * SLOT + block % per_term * PIVOTS
        span = range(PIVOTS)
        columns = [jnp.broadcast_to(system[:, p + j : p + j + 1], shape) for j in span]
        rows = [system[p + i : p + i + 1, :] for i in span]
        entry = [[columns[j][p + i : p + i + 1, :] for j in span] for i in span]
        for i in span:
            inverse = 1.0 / entry[i][i]
            rows[i] = rows[i] * inverse
            for j in range(i + 1, PIVOTS):
                entry[i][j] = entry[i][j] * inverse
            for m in span:
                if m != i:
                    rows[m] = rows[m] - entry[m][i] * rows[i]
                    for j in range(i + 1, PIVOTS):
                        entry[m][j] = entry[m][j] - entry[m][i] * entry[i][j]
        for j in span:
            system = system - columns[j] * rows[j]
        for i in span:
            system = jnp.where(row == p + i, rows[i], system)
    return jnp.broadcast_to(system[:, 3 * SLOT : 3 * SLOT + 1], shape)


def difference_kernel(
    count,
    part,
    shifted,
    rest,
    across_table,
    table,
    out,
    across,
    coefficients,
    basis,
    recv,
    send_sem,
    recv_sem,
):
    pixels = rest.shape[0]
    total_rows = float(count * pixels)
    me = lax.axis_index("quad")
    greet("quad", count, me)
    copies = []
    for step in range(1, count):
        copy = pltpu.make_async_remote_copy(
            src_ref=part,
            dst_ref=recv.at[step - 1],
            send_sem=send_sem.at[step - 1],
            recv_sem=recv_sem.at[step - 1],
            device_id={"quad": lax.rem(me + step, count)},
            device_id_type=pl.DeviceIdType.MESH,
        )
        copy.start()
        copies.append(copy)

    for f in range(NFACT):
        across[f, 0:ROWPAD, :] = jnp.zeros((ROWPAD, pixels), jnp.bfloat16)
        across[f, ROWPAD + pixels :, :] = jnp.zeros((ROWPAD, pixels), jnp.bfloat16)

    def across_step(tile, carry):
        first = pl.multiple_of(tile * TILE, TILE)
        source = shifted[:, pl.ds(first, 2 * TILE)]
        for pair in range(0, NFACT, 2):
            last = min(pair + 2, NFACT)
            value = jnp.dot(
                source,
                across_table[:, pair * TILE : last * TILE],
                preferred_element_type=jnp.float32,
            ).astype(jnp.bfloat16)
            for f in range(pair, last):
                across[f, ROWPAD : ROWPAD + pixels, pl.ds(first, TILE)] = value[
                    :, (f - pair) * TILE : (f - pair + 1) * TILE
                ]
        return carry

    lax.fori_loop(0, pixels // TILE, across_step, 0)

    normal = part[...]
    for step, copy in enumerate(copies):
        copy.wait()
        normal = normal + recv[step]
    coefficients[...] = solve(normal)
    tiles = pixels // TILE
    lane = lax.broadcasted_iota(jnp.int32, (8, pixels), 1).astype(jnp.float32)
    side = (lane + 0.5) / pixels * 2.0 - 1.0
    sub = lax.broadcasted_iota(jnp.int32, (8, TILE), 0)

    def tile_step(tile, carry):
        first = pl.multiple_of(tile * TILE, TILE)
        start = 0
        for f in range(NFACT):
            count = len(BY_ACROSS[f]) * TILE
            basis[start : start + count, :] = jnp.dot(
                table[start : start + count, :],
                across[f, pl.ds(first, 2 * TILE), :],
                preferred_element_type=jnp.float32,
            )
            start += count

        def row_step(chunk, inner):
            rows = pl.multiple_of(chunk * 8, 8)
            number = (me * pixels + first + rows + sub).astype(jnp.float32)
            up = (number + 0.5) / total_rows * 2.0 - 1.0

            def terms(k):
                flat = coefficients[k : k + 1, :] + up * coefficients[SLOT + k : SLOT + k + 1, :]
                slope = jnp.broadcast_to(
                    coefficients[2 * SLOT + k : 2 * SLOT + k + 1, :], (8, TILE)
                )
                wide = pixels // TILE
                return jnp.concatenate([flat] * wide, 1), jnp.concatenate([slope] * wide, 1)

            flat_sum, slope_sum = terms(NBASIS)
            for index, k in enumerate([k for ks in BY_ACROSS for k in ks]):
                value = basis[pl.ds(index * TILE + rows, 8), :]
                flat, slope = terms(k)
                flat_sum = flat_sum + value * flat
                slope_sum = slope_sum + value * slope
            here = pl.ds(pl.multiple_of(first + rows, 8), 8)
            out[here, :] = rest[here, :] - (flat_sum + side * slope_sum)
            return inner

        lax.fori_loop(0, TILE // 8, row_step, 0)
        return carry

    lax.fori_loop(0, tiles, tile_step, 0)


def difference_image(part, shifted, rest, count):
    pixels = rest.shape[0]
    vmem = pl.BlockSpec(memory_space=pltpu.VMEM)
    across_table, _, _, table = tables()
    return pl.pallas_call(
        functools.partial(difference_kernel, count),
        out_shape=jax.ShapeDtypeStruct((pixels, pixels), jnp.float32),
        in_specs=[vmem] * 5,
        out_specs=vmem,
        scratch_shapes=[
            pltpu.VMEM((NFACT, pixels + 2 * ROWPAD, pixels), jnp.bfloat16),
            pltpu.VMEM((3 * SLOT, TILE), jnp.float32),
            pltpu.VMEM((NBASIS * TILE, pixels), jnp.float32),
            pltpu.VMEM((count - 1,) + part.shape, jnp.float32),
            pltpu.SemaphoreType.DMA((count - 1,)),
            pltpu.SemaphoreType.DMA((count - 1,)),
        ],
        compiler_params=pltpu.CompilerParams(
            collective_id=1, has_side_effects=True, vmem_limit_bytes=DIFFERENCE_VMEM
        ),
        name="difference",
    )(part, shifted, rest, jnp.asarray(across_table), jnp.asarray(table))


def local(template_patches, intersection, offsets, science, weight, positions):
    ccds = lax.axis_size("ccd")
    quads = lax.axis_size("quad")
    pixels = science.shape[-1]
    total_rows = float(quads * pixels)
    wanted = intersection[:, 0]
    bands = cut_bands(wanted, offsets[:, 0], template_patches[0, 0], ccds)
    bands = exchange_bands(bands, ccds)
    shifted, normal, rest = normal_equations(
        wanted, positions[0, 0].T, bands, science[0, 0], weight[0, 0], total_rows
    )
    image = difference_image(normal, shifted, rest, quads)
    return image[None, None]


def solution(mesh):
    return jax.shard_map(
        local,
        mesh=mesh,
        in_specs=(
            P("ccd", "quad", None, None),
            P(None, "quad", None),
            P(None, "quad", None),
            P("ccd", "quad", None, None),
            P("ccd", "quad", None, None),
            P("ccd", "quad", None, None),
        ),
        out_specs=P("ccd", "quad", None, None),
        check_vma=False,
    )
```

```python
import functools

import jax
import jax.numpy as jnp
import ml_dtypes
import numpy as np
from jax import lax
from jax.experimental import pallas as pl
from jax.experimental.pallas import tpu as pltpu
from jax.sharding import PartitionSpec as P

BANDS = 8
RADIUS = 10
NBASIS = 27
NCOEF = 84
STAMP = 32
NSTAMP = 32
NFACT = 11
TILE = 128
SLOT = 32
SLAB = 64
MARGIN = 16
ROWPAD = 64
GROUP = 4
CHUNK = 8
PIVOTS = 4
NORMAL_VMEM = 24 * 2**20
DIFFERENCE_VMEM = 30 * 2**20

kernel_widths = (0.75, 1.5, 3.0)
poly_degrees = (4, 2, 2)
ridge_share = 0.02


def factor_taps():
    tap_offsets = np.arange(-RADIUS, RADIUS + 1, dtype=np.float64)
    factor_rows = []
    for kernel_width, degree in zip(kernel_widths, poly_degrees):
        scaled = tap_offsets / kernel_width
        for exponent in range(degree + 1):
            values = scaled**exponent * np.exp(-0.5 * scaled * scaled)
            factor_rows.append(values / np.sqrt(np.sum(values * values)))
    return np.stack(factor_rows).astype(np.float32).astype(ml_dtypes.bfloat16)


def kernel_list():
    pairs = []
    first_slot = 0
    for degree in poly_degrees:
        for down in range(degree + 1):
            for across in range(degree - down + 1):
                pairs.append((first_slot + down, first_slot + across))
        first_slot += degree + 1
    return pairs


PAIRS = kernel_list()
BY_ACROSS = [[k for k, (_, across) in enumerate(PAIRS) if across == f] for f in range(NFACT)]


def banded(taps, n_in, n_out, shift):
    offset = np.arange(n_in)[:, None] - shift - np.arange(n_out)[None, :]
    inside = np.abs(offset) <= RADIUS
    return np.where(inside, taps[np.clip(offset + RADIUS, 0, 2 * RADIUS)], 0)


@functools.lru_cache(None)
def tables():
    taps = factor_taps().astype(np.float32)
    across = np.concatenate([banded(t, 2 * TILE, TILE, ROWPAD) for t in taps], 1)
    stamp_across = np.zeros((GROUP * SLAB, NFACT * TILE), np.float32)
    for f in range(NFACT):
        block = banded(taps[f], SLAB, STAMP, MARGIN)
        for j in range(GROUP):
            stamp_across[
                j * SLAB : (j + 1) * SLAB, f * TILE + j * STAMP : f * TILE + (j + 1) * STAMP
            ] = block
    stamp_down = np.zeros((STAMP, SLOT, NFACT, SLAB), np.float32)
    for k, (down, f) in enumerate(PAIRS):
        stamp_down[:, k, f, :] = banded(taps[down], SLAB, STAMP, MARGIN).T
    stamp_down = stamp_down.reshape(STAMP * SLOT, NFACT * SLAB)
    down = np.concatenate(
        [banded(taps[PAIRS[k][0]], 2 * TILE, TILE, ROWPAD).T for ks in BY_ACROSS for k in ks], 0
    )
    return tuple(t.astype(ml_dtypes.bfloat16) for t in (across, stamp_across, stamp_down, down))


def rows_from(ref, first, count, lanes):
    start = jnp.minimum(lax.div(first, 8) * 8, ref.shape[0] - count - 8)
    start = pl.multiple_of(start, 8)
    value = ref[pl.ds(start, count + 8), lanes]
    turn = lax.rem(count + 8 - (first - start), count + 8)
    return pltpu.roll(value, turn, 0)[:count]


def greet(axis, count, me):
    barrier = pltpu.get_barrier_semaphore()
    for step in range(1, count):
        pl.semaphore_signal(
            barrier,
            inc=1,
            device_id={axis: lax.rem(me + step, count)},
            device_id_type=pl.DeviceIdType.MESH,
        )
    pl.semaphore_wait(barrier, count - 1)


def cut_kernel(count, band_rows, wanted, starts, patch, bands):
    me = lax.axis_index("ccd")
    for target in range(count):
        first = jnp.int32(0)
        for b in range(BANDS):
            first = first + jnp.where(wanted[target, b] == me, starts[target, b], 0)
        bands[target] = rows_from(patch, first, band_rows, slice(None))


def cut_bands(wanted, starts, patch, count):
    pixels = patch.shape[0]
    band_rows = pixels // BANDS
    vmem = pl.BlockSpec(memory_space=pltpu.VMEM)
    smem = pl.BlockSpec(memory_space=pltpu.SMEM)
    return pl.pallas_call(
        functools.partial(cut_kernel, count, band_rows),
        out_shape=jax.ShapeDtypeStruct((count, band_rows, pixels), jnp.float32),
        in_specs=[smem, smem, vmem],
        out_specs=vmem,
        name="band_cut",
    )(wanted, starts, patch)


def exchange_kernel(count, bands, recv, send_sem, recv_sem, own_sem):
    me = lax.axis_index("ccd")
    own = pltpu.make_async_copy(bands.at[me], recv.at[me], own_sem)
    own.start()
    greet("ccd", count, me)
    copies = []
    for step in range(1, count):
        target = lax.rem(me + step, count)
        copy = pltpu.make_async_remote_copy(
            src_ref=bands.at[target],
            dst_ref=recv.at[me],
            send_sem=send_sem.at[step - 1],
            recv_sem=recv_sem.at[step - 1],
            device_id={"ccd": target},
            device_id_type=pl.DeviceIdType.MESH,
        )
        copy.start()
        copies.append(copy)
    for copy in copies:
        copy.wait()
    own.wait()


def exchange_bands(bands, count):
    return pl.pallas_call(
        functools.partial(exchange_kernel, count),
        out_shape=jax.ShapeDtypeStruct(bands.shape, jnp.float32),
        in_specs=[pl.BlockSpec(memory_space=pl.ANY)],
        out_specs=pl.BlockSpec(memory_space=pl.ANY),
        scratch_shapes=[
            pltpu.SemaphoreType.DMA((count - 1,)),
            pltpu.SemaphoreType.DMA((count - 1,)),
            pltpu.SemaphoreType.DMA,
        ],
        compiler_params=pltpu.CompilerParams(collective_id=0, has_side_effects=True),
        cost_estimate=pl.CostEstimate(flops=0, bytes_accessed=50 * 2**20, transcendentals=0),
        name="band_exchange",
    )(bands)


def normal_kernel(
    total_rows,
    wanted,
    corners,
    bands,
    science,
    weight,
    stamp_table,
    down_table,
    shifted,
    normal,
    rest,
    padded,
    slab_in,
    slab,
    root_weight,
    residual,
    up,
    side,
    halves,
):
    pixels = science.shape[0]
    band_rows = pixels // BANDS
    me = lax.axis_index("ccd")
    quad = lax.axis_index("quad")
    padded[...] = jnp.zeros_like(padded)
    for b in range(BANDS):
        rows = slice(b * band_rows, (b + 1) * band_rows)
        band = bands[wanted[me, b]]
        padded[MARGIN + b * band_rows : MARGIN + (b + 1) * band_rows, TILE : TILE + pixels] = band
        rest[rows, :] = science[rows, :] - band
    lane_slab = lax.broadcasted_iota(jnp.int32, (SLAB, GROUP * SLAB), 1) // SLAB
    lane_stamp = lax.broadcasted_iota(jnp.int32, (STAMP, TILE), 1) // STAMP
    lane_in = lax.broadcasted_iota(jnp.int32, (STAMP, TILE), 1) % STAMP
    row_in = lax.broadcasted_iota(jnp.int32, (STAMP, TILE), 0)

    for group in range(NSTAMP // GROUP):
        slab_value = jnp.zeros((SLAB, GROUP * SLAB), jnp.float32)
        rest_value = jnp.zeros((STAMP, TILE), jnp.float32)
        weight_value = jnp.zeros((STAMP, TILE), jnp.float32)
        row_of = jnp.zeros((STAMP, TILE), jnp.int32)
        col_of = jnp.zeros((STAMP, TILE), jnp.int32)
        for j in range(GROUP):
            top = corners[0, group * GROUP + j]
            left = corners[1, group * GROUP + j]
            first = left + (TILE - MARGIN)
            tile = pl.multiple_of(lax.div(first, TILE) * TILE, TILE)
            wide = rows_from(padded, top, SLAB, pl.ds(tile, 2 * TILE))
            wide = pltpu.roll(wide, lax.rem(j * SLAB - (first - tile) + 2 * TILE, 2 * TILE), 1)
            slab_value = jnp.where(lane_slab == j, wide, slab_value)
            tile = pl.multiple_of(lax.div(left, TILE) * TILE, TILE)
            turn = lax.rem(j * STAMP - (left - tile) + TILE, TILE)
            here = lane_stamp == j

            def cut(ref, before):
                piece = pltpu.roll(rows_from(ref, top, STAMP, pl.ds(tile, TILE)), turn, 1)
                return jnp.where(here, piece, before)

            rest_value = cut(rest, rest_value)
            weight_value = cut(weight, weight_value)
            row_of = jnp.where(here, top, row_of)
            col_of = jnp.where(here, left, col_of)
        slab_in[group * SLAB : (group + 1) * SLAB, :] = slab_value.astype(jnp.bfloat16)
        lanes = slice(group * TILE, (group + 1) * TILE)
        root_weight[:, lanes] = jnp.sqrt(weight_value)
        residual[:, lanes] = rest_value
        rows = (row_of + row_in + quad * pixels).astype(jnp.float32)
        up[:, lanes] = (rows + 0.5) / total_rows * 2.0 - 1.0
        columns = (col_of + lane_in).astype(jnp.float32)
        side[:, lanes] = (columns + 0.5) / pixels * 2.0 - 1.0

    groups = NSTAMP // GROUP
    for pair in range(0, NFACT, 2):
        last = min(pair + 2, NFACT)
        part = jnp.dot(
            slab_in[...],
            stamp_table[:, pair * TILE : last * TILE],
            preferred_element_type=jnp.float32,
        ).astype(jnp.bfloat16)
        for f in range(pair, last):
            for group in range(groups):
                slab[f * SLAB : (f + 1) * SLAB, group * TILE : (group + 1) * TILE] = part[
                    group * SLAB : (group + 1) * SLAB, (f - pair) * TILE : (f - pair + 1) * TILE
                ]

    width = NSTAMP * STAMP
    feature = lax.broadcasted_iota(jnp.int32, (SLOT, width), 0)
    halves[...] = jnp.zeros_like(halves)

    def chunk_step(chunk, total):
        first = pl.multiple_of(chunk * (CHUNK * SLOT), CHUNK * SLOT)
        values = jnp.dot(
            down_table[pl.ds(first, CHUNK * SLOT), :],
            slab[...],
            preferred_element_type=jnp.float32,
        )
        row0 = pl.multiple_of(chunk * CHUNK, CHUNK)
        roots = root_weight[pl.ds(row0, CHUNK), :]
        rests = residual[pl.ds(row0, CHUNK), :]
        ups = up[pl.ds(row0, CHUNK), :]
        sides = side[pl.ds(row0, CHUNK), :]
        for a in range(CHUNK):
            lanes = slice(a * width, (a + 1) * width)
            basis = values[a * SLOT : (a + 1) * SLOT]
            basis = jnp.where(feature == NBASIS, 1.0, basis)
            basis = jnp.where(feature == NBASIS + 1, rests[a : a + 1], basis)
            basis = basis * roots[a : a + 1]
            for s, term in enumerate((basis, basis * ups[a : a + 1], basis * sides[a : a + 1])):
                high = term.astype(jnp.bfloat16)
                low = (term - high.astype(jnp.float32)).astype(jnp.bfloat16)
                halves[s * SLOT : (s + 1) * SLOT, lanes] = high
                halves[TILE + s * SLOT : TILE + (s + 1) * SLOT, lanes] = low
        return total + lax.dot_general(
            halves[0 : 3 * SLOT, :],
            halves[...],
            (((1,), (1,)), ((), ())),
            preferred_element_type=jnp.float32,
        )

    total = lax.fori_loop(
        0, STAMP // CHUNK, chunk_step, jnp.zeros((3 * SLOT, 2 * TILE), jnp.float32)
    )
    mixed = jnp.concatenate([total[:, TILE:], jnp.zeros((TILE - 3 * SLOT, TILE), jnp.float32)], 0)
    normal[...] = total[:, :TILE] + total[:, TILE:] + mixed.T[: 3 * SLOT]

    turned = pltpu.roll(padded[MARGIN : MARGIN + pixels, :], padded.shape[1] - ROWPAD, 1)
    shifted[...] = turned[:, : pixels + 2 * ROWPAD].astype(jnp.bfloat16)


def normal_equations(wanted, corners, bands, science, weight, total_rows):
    pixels = science.shape[0]
    _, stamp_table, down_table, _ = tables()
    width = NSTAMP * STAMP
    vmem = pl.BlockSpec(memory_space=pltpu.VMEM)
    smem = pl.BlockSpec(memory_space=pltpu.SMEM)
    return pl.pallas_call(
        functools.partial(normal_kernel, total_rows),
        out_shape=(
            jax.ShapeDtypeStruct((pixels, pixels + 2 * ROWPAD), jnp.bfloat16),
            jax.ShapeDtypeStruct((3 * SLOT, TILE), jnp.float32),
            jax.ShapeDtypeStruct((pixels, pixels), jnp.float32),
        ),
        in_specs=[smem, smem] + [vmem] * 5,
        out_specs=(vmem, vmem, vmem),
        scratch_shapes=[
            pltpu.VMEM((pixels + 3 * MARGIN, pixels + 2 * TILE), jnp.float32),
            pltpu.VMEM((NSTAMP // GROUP * SLAB, GROUP * SLAB), jnp.bfloat16),
            pltpu.VMEM((NFACT * SLAB, width), jnp.bfloat16),
            pltpu.VMEM((STAMP, width), jnp.float32),
            pltpu.VMEM((STAMP, width), jnp.float32),
            pltpu.VMEM((STAMP, width), jnp.float32),
            pltpu.VMEM((STAMP, width), jnp.float32),
            pltpu.VMEM((2 * TILE, CHUNK * width), jnp.bfloat16),
        ],
        compiler_params=pltpu.CompilerParams(vmem_limit_bytes=NORMAL_VMEM),
        name="normal_equations",
    )(
        wanted,
        corners,
        bands,
        science,
        weight,
        jnp.asarray(stamp_table),
        jnp.asarray(down_table),
    )


def solve(normal):
    shape = normal.shape
    row = lax.broadcasted_iota(jnp.int32, shape, 0)
    lane = lax.broadcasted_iota(jnp.int32, shape, 1)
    row_used = row % SLOT <= NBASIS
    used = row_used & (lane % SLOT <= NBASIS) & (lane < 3 * SLOT)
    diagonal = row == lane
    trace = jnp.sum(jnp.where(used & diagonal, normal, 0.0))
    ridge = ridge_share * trace / NCOEF
    vector = jnp.sum(
        jnp.where((lane == NBASIS + 1) & row_used, normal, 0.0), axis=1, keepdims=True
    )
    system = jnp.where(used, normal, 0.0)
    system = system + jnp.where(diagonal, jnp.where(row_used, ridge, 1.0), 0.0)
    system = jnp.where(lane == 3 * SLOT, vector, system)
    for block in range(NCOEF // PIVOTS):
        per_term = (NBASIS + 1) // PIVOTS
        p = block // per_term * SLOT + block % per_term * PIVOTS
        span = range(PIVOTS)
        columns = [jnp.broadcast_to(system[:, p + j : p + j + 1], shape) for j in span]
        rows = [system[p + i : p + i + 1, :] for i in span]
        entry = [[columns[j][p + i : p + i + 1, :] for j in span] for i in span]
        for i in span:
            inverse = 1.0 / entry[i][i]
            rows[i] = rows[i] * inverse
            for j in range(i + 1, PIVOTS):
                entry[i][j] = entry[i][j] * inverse
            for m in span:
                if m != i:
                    rows[m] = rows[m] - entry[m][i] * rows[i]
                    for j in range(i + 1, PIVOTS):
                        entry[m][j] = entry[m][j] - entry[m][i] * entry[i][j]
        for j in span:
            system = system - columns[j] * rows[j]
        for i in span:
            system = jnp.where(row == p + i, rows[i], system)
    return jnp.broadcast_to(system[:, 3 * SLOT : 3 * SLOT + 1], shape)


def difference_kernel(
    count,
    part,
    shifted,
    rest,
    across_table,
    table,
    out,
    across,
    coefficients,
    basis,
    recv,
    send_sem,
    recv_sem,
):
    pixels = rest.shape[0]
    total_rows = float(count * pixels)
    me = lax.axis_index("quad")
    greet("quad", count, me)
    copies = []
    for step in range(1, count):
        copy = pltpu.make_async_remote_copy(
            src_ref=part,
            dst_ref=recv.at[step - 1],
            send_sem=send_sem.at[step - 1],
            recv_sem=recv_sem.at[step - 1],
            device_id={"quad": lax.rem(me + step, count)},
            device_id_type=pl.DeviceIdType.MESH,
        )
        copy.start()
        copies.append(copy)

    for f in range(NFACT):
        across[f, 0:ROWPAD, :] = jnp.zeros((ROWPAD, pixels), jnp.bfloat16)
        across[f, ROWPAD + pixels :, :] = jnp.zeros((ROWPAD, pixels), jnp.bfloat16)

    def across_step(tile, carry):
        first = pl.multiple_of(tile * TILE, TILE)
        source = shifted[:, pl.ds(first, 2 * TILE)]
        for pair in range(0, NFACT, 2):
            last = min(pair + 2, NFACT)
            value = jnp.dot(
                source,
                across_table[:, pair * TILE : last * TILE],
                preferred_element_type=jnp.float32,
            ).astype(jnp.bfloat16)
            for f in range(pair, last):
                across[f, ROWPAD : ROWPAD + pixels, pl.ds(first, TILE)] = value[
                    :, (f - pair) * TILE : (f - pair + 1) * TILE
                ]
        return carry

    lax.fori_loop(0, pixels // TILE, across_step, 0)

    normal = part[...]
    for step, copy in enumerate(copies):
        copy.wait()
        normal = normal + recv[step]
    coefficients[...] = solve(normal)
    tiles = pixels // TILE
    lane = lax.broadcasted_iota(jnp.int32, (8, pixels), 1).astype(jnp.float32)
    side = (lane + 0.5) / pixels * 2.0 - 1.0
    sub = lax.broadcasted_iota(jnp.int32, (8, TILE), 0)

    def tile_step(tile, carry):
        first = pl.multiple_of(tile * TILE, TILE)
        start = 0
        for f in range(NFACT):
            count = len(BY_ACROSS[f]) * TILE
            basis[start : start + count, :] = jnp.dot(
                table[start : start + count, :],
                across[f, pl.ds(first, 2 * TILE), :],
                preferred_element_type=jnp.float32,
            )
            start += count

        def row_step(chunk, inner):
            rows = pl.multiple_of(chunk * 8, 8)
            number = (me * pixels + first + rows + sub).astype(jnp.float32)
            up = (number + 0.5) / total_rows * 2.0 - 1.0

            def terms(k):
                flat = coefficients[k : k + 1, :] + up * coefficients[SLOT + k : SLOT + k + 1, :]
                slope = jnp.broadcast_to(
                    coefficients[2 * SLOT + k : 2 * SLOT + k + 1, :], (8, TILE)
                )
                wide = pixels // TILE
                return jnp.concatenate([flat] * wide, 1), jnp.concatenate([slope] * wide, 1)

            flat_sum, slope_sum = terms(NBASIS)
            for index, k in enumerate([k for ks in BY_ACROSS for k in ks]):
                value = basis[pl.ds(index * TILE + rows, 8), :]
                flat, slope = terms(k)
                flat_sum = flat_sum + value * flat
                slope_sum = slope_sum + value * slope
            here = pl.ds(pl.multiple_of(first + rows, 8), 8)
            out[here, :] = rest[here, :] - (flat_sum + side * slope_sum)
            return inner

        lax.fori_loop(0, TILE // 8, row_step, 0, unroll=2)
        return carry

    lax.fori_loop(0, tiles, tile_step, 0)


def difference_image(part, shifted, rest, count):
    pixels = rest.shape[0]
    vmem = pl.BlockSpec(memory_space=pltpu.VMEM)
    across_table, _, _, table = tables()
    return pl.pallas_call(
        functools.partial(difference_kernel, count),
        out_shape=jax.ShapeDtypeStruct((pixels, pixels), jnp.float32),
        in_specs=[vmem] * 5,
        out_specs=vmem,
        scratch_shapes=[
            pltpu.VMEM((NFACT, pixels + 2 * ROWPAD, pixels), jnp.bfloat16),
            pltpu.VMEM((3 * SLOT, TILE), jnp.float32),
            pltpu.VMEM((NBASIS * TILE, pixels), jnp.float32),
            pltpu.VMEM((count - 1,) + part.shape, jnp.float32),
            pltpu.SemaphoreType.DMA((count - 1,)),
            pltpu.SemaphoreType.DMA((count - 1,)),
        ],
        compiler_params=pltpu.CompilerParams(
            collective_id=1, has_side_effects=True, vmem_limit_bytes=DIFFERENCE_VMEM
        ),
        name="difference",
    )(part, shifted, rest, jnp.asarray(across_table), jnp.asarray(table))


def local(template_patches, intersection, offsets, science, weight, positions):
    ccds = lax.axis_size("ccd")
    quads = lax.axis_size("quad")
    pixels = science.shape[-1]
    total_rows = float(quads * pixels)
    wanted = intersection[:, 0]
    bands = cut_bands(wanted, offsets[:, 0], template_patches[0, 0], ccds)
    bands = exchange_bands(bands, ccds)
    shifted, normal, rest = normal_equations(
        wanted, positions[0, 0].T, bands, science[0, 0], weight[0, 0], total_rows
    )
    image = difference_image(normal, shifted, rest, quads)
    return image[None, None]


def solution(mesh):
    return jax.shard_map(
        local,
        mesh=mesh,
        in_specs=(
            P("ccd", "quad", None, None),
            P(None, "quad", None),
            P(None, "quad", None),
            P("ccd", "quad", None, None),
            P("ccd", "quad", None, None),
            P("ccd", "quad", None, None),
        ),
        out_specs=P("ccd", "quad", None, None),
        check_vma=False,
    )
```
